128 devices in a mesh: dp: 8 (over z, core), mp: 16 (over y, x).
Axes of the slice: x: 4, y: 4, z: 4, core: 2. Of those that a mesh axis runs over, the one named last changes fastest.
Arguments:
- hidden: bfloat16 [4, 1024, 8192], P(None, 'dp'), may hold values from -6 to 6
- out_grads: bfloat16 [1024, 24576], P('dp', 'mp'), may hold values from -0.4375 to 0.4375
- mask_words: int32 [512, 24576], P(None, 'mp'), may hold values from 0 to 2925, as said below
- owner: int32 [16, 48], P('dp', 'mp'), may hold values from 0 to 15, as said below
- left_root: bfloat16 [1536, 512, 512], P(('dp', 'mp')), may hold values from -1 to 5, as said below
- right_root: bfloat16 [1536, 512, 512], P(('dp', 'mp')), may hold values from -1 to 5, as said below
Outputs:
- update: bfloat16 [8192, 24576], P('dp', 'mp')
The draws below stay inside these ranges and needn't reach their ends.
Inputs may be any that keep to these rules, and one draw needn't show every extreme that they name: Each block's owner is an index along mp within the block's own dp row. A device hands at most 1 of its blocks to one owner, and some device does so in every dp row; every owner receives at least one block, none more than 12, and in every dp row one owner receives exactly 12. `mask_words`: every word holds four codes in base 8, each 0 to 5. `left_root`: symmetric matrices. `right_root`: symmetric matrices.
All inputs are finite; a program needn't handle non-finite values.
Results may differ from the reference program's by a relative error of at most 0.02.
Values may be sent and summed in bfloat16 or wider, within the bound.
A program may use at most 256 MiB of HBM per device.

```python
import jax
import jax.numpy as jnp
from jax import lax

D = 6144
FF = 8192
BLOCK = 512
EXPERTS = 4
TOKENS = 1024
BR_DEV = 2
BC_DEV = 3
NB_DEV = 6
CAPO = 12
N_DP = 8
N_MP = 16
DEVICES = 128


def draw_mask_words(key, part):
    key = jax.random.fold_in(key, 11)
    codes_key, first_key, second_key = jax.random.split(key, 3)
    column_total = EXPERTS * D
    group_codes = jax.random.randint(codes_key, (FF // 16, column_total, 4), 0, 6, dtype=jnp.int32)
    low_column = jax.random.randint(first_key, (), 0, column_total, dtype=jnp.int32)
    step_column = jax.random.randint(second_key, (), 1, column_total, dtype=jnp.int32)
    high_column = (low_column + step_column) % column_total
    column_index = jnp.arange(column_total, dtype=jnp.int32)
    first_row = jnp.arange(FF // 16, dtype=jnp.int32)[:, None] == 0
    at_low = (first_row & (column_index[None, :] == low_column))[:, :, None]
    at_high = (first_row & (column_index[None, :] == high_column))[:, :, None]
    group_codes = jnp.where(at_low, 0, group_codes)
    group_codes = jnp.where(at_high, 5, group_codes)
    powers = 8 ** jnp.arange(4, dtype=jnp.int32)
    return jnp.sum(group_codes * powers, axis=2).astype(jnp.int32)


def draw_owner(key, part):
    key = jax.random.fold_in(key, 23)
    slot_total = N_MP * NB_DEV
    remainder = slot_total - CAPO - (N_MP - 1)
    position = jnp.arange(slot_total, dtype=jnp.int32)
    tables = []
    for replica_row in range(N_DP):
        row_key = jax.random.fold_in(key, replica_row)
        order_key, weight_key, offset_key = jax.random.split(row_key, 3)
        order = jax.random.permutation(order_key, N_MP).astype(jnp.int32)
        weights = jax.random.randint(weight_key, (N_MP - 1,), 3, 5, dtype=jnp.int32)
        weight_total = jnp.sum(weights)
        shares = weights * remainder // weight_total
        leftover = remainder - jnp.sum(shares)
        others = 1 + shares + (jnp.arange(N_MP - 1, dtype=jnp.int32) < leftover).astype(jnp.int32)
        owner_loads = jnp.concatenate([jnp.full((1,), CAPO, jnp.int32), others])
        load_ends = jnp.cumsum(owner_loads)
        owner_rank = jnp.sum((load_ends[None, :] <= position[:, None]).astype(jnp.int32), axis=1)
        sequence = order[owner_rank]
        offset = jax.random.randint(offset_key, (), 0, slot_total, dtype=jnp.int32)
        rotated = sequence[(position + offset) % slot_total]
        tables.append(rotated.reshape(NB_DEV, N_MP).T)
    owner_grid = jnp.stack(tables).reshape(N_DP, N_MP, BR_DEV, BC_DEV).transpose(0, 2, 1, 3)
    return owner_grid.reshape(N_DP * BR_DEV, N_MP * BC_DEV).astype(jnp.int32)


def root_matrices(key, lowest, highest):
    normal_key, diagonal_key = jax.random.split(key)
    count = DEVICES * CAPO
    normals = jnp.clip(jax.random.normal(normal_key, (count, BLOCK, BLOCK), jnp.float32), -4.0, 4.0)
    symmetric = (normals + jnp.swapaxes(normals, 1, 2)) * (0.3 / BLOCK ** 0.5)
    logs = jax.random.uniform(diagonal_key, (count, BLOCK, 1), jnp.float32, jnp.log(lowest), jnp.log(highest))
    identity = jnp.eye(BLOCK, dtype=jnp.float32)[None]
    return (symmetric + jnp.exp(logs) * identity).astype(jnp.bfloat16)


def draw_left_root(key, part):
    key = jax.random.fold_in(key, 31)
    return root_matrices(key, 1.0, 3.0)


def draw_right_root(key, part):
    key = jax.random.fold_in(key, 37)
    return root_matrices(key, 1.0, 3.0)


def steps_of(rng, dims, shards, low, high):
    level = 1.0
    for dim, parts in shards:
        heights = jax.random.uniform(jax.random.fold_in(jax.random.fold_in(rng, 6), dim), (parts,), jnp.float32, low / len(shards), high / len(shards))
        level = level * jnp.repeat(jnp.exp(heights), dims[dim] // parts).reshape((-1,) + (1,) * (len(dims) - 1 - dim))
    return level


def scatter_about(key, shape, width, most, cuts=(), kind=jnp.bfloat16):
    entries = jax.random.normal(key, shape, jnp.float32) * width
    if len(cuts) > 0:
        entries = steps_of(key, shape, cuts, -0.22, 0.18) * entries
    return jnp.clip(entries, min=-most, max=most).astype(kind)


def setup_inputs(seed: int = 0) -> dict:
    seeds = jax.random.split(jax.random.key(seed), 7)
    return {
        "hidden": scatter_about(seeds[0], (EXPERTS, TOKENS, FF), 1.0, 6.0, ((1, 8),)),
        "out_grads": scatter_about(seeds[1], (TOKENS, EXPERTS * D), 0.03, 0.4375, ((0, 8), (1, 16))),
        "mask_words": draw_mask_words(jax.random.fold_in(seeds[6], 71), 0),
        "owner": draw_owner(jax.random.fold_in(seeds[6], 71), 0),
        "left_root": draw_left_root(jax.random.fold_in(seeds[6], 71), 0),
        "right_root": draw_right_root(jax.random.fold_in(seeds[6], 71), 0),
    }


def decode_codes(mask_words):
    powers = 8 ** jnp.arange(4, dtype=jnp.int32)
    group_codes = mask_words[:, None, :] // powers[None, :, None] % 8
    return group_codes.reshape(mask_words.shape[0] * 4, mask_words.shape[1])

def kept_selectors(group_codes):
    first_kept = jnp.where(group_codes >= 3, jnp.where(group_codes >= 5, 2, 1), 0)
    second_kept = jnp.where(group_codes == 0, 1, jnp.where((group_codes == 1) | (group_codes == 3), 2, 3))
    lane_index = jnp.arange(4, dtype=jnp.int32)[None, :, None]
    select_first = (lane_index == first_kept[:, None, :]).astype(jnp.float32)
    select_second = (lane_index == second_kept[:, None, :]).astype(jnp.float32)
    return (select_first, select_second)

def pack_rows(dense_rows, group_codes):
    select_first, select_second = kept_selectors(group_codes)
    grouped = dense_rows.reshape(group_codes.shape[0], 4, dense_rows.shape[1])
    kept_first = lax.optimization_barrier(jnp.sum(grouped * select_first, axis=1))
    kept_second = lax.optimization_barrier(jnp.sum(grouped * select_second, axis=1))
    return jnp.stack([kept_first, kept_second], axis=1).reshape(-1, dense_rows.shape[1])

def unpack_rows(packed_rows, group_codes):
    select_first, select_second = kept_selectors(group_codes)
    paired = packed_rows.reshape(group_codes.shape[0], 2, packed_rows.shape[1])
    dense_rows = paired[:, 0:1, :] * select_first + paired[:, 1:2, :] * select_second
    return dense_rows.reshape(-1, packed_rows.shape[1])

def precondition_one(grad_block, left_block, right_block):
    right_applied = jnp.dot(grad_block.astype(jnp.float32), right_block.astype(jnp.float32)).astype(jnp.bfloat16)
    preconditioned = jnp.dot(left_block.astype(jnp.float32), right_applied.astype(jnp.float32))
    grad_float = grad_block.astype(jnp.float32)
    numerator = jnp.sqrt(jnp.mean(grad_float * grad_float))
    denominator = jnp.sqrt(jnp.mean(preconditioned * preconditioned) + 1e-06)
    return (preconditioned * (numerator / denominator)).astype(jnp.bfloat16)

def reference(hidden, out_grads, mask_words, owner, left_root, right_root):
    tok_rows = TOKENS // N_DP
    group_codes = decode_codes(mask_words)

    def add_replica(replica, summed):
        begin = (replica * tok_rows).astype(jnp.int32)
        pieces = []
        for expert in range(EXPERTS):
            activations = lax.dynamic_slice_in_dim(hidden[expert], begin, tok_rows, 0)
            output_rows = lax.dynamic_slice_in_dim(out_grads[:, expert * D:(expert + 1) * D], begin, tok_rows, 0)
            pieces.append(jnp.dot(activations.T, output_rows, preferred_element_type=jnp.float32))
        dense_rows = jnp.concatenate(pieces, axis=1)
        packed = pack_rows(dense_rows, group_codes).astype(jnp.bfloat16)
        return summed + packed.astype(jnp.float32)
    summed = lax.fori_loop(jnp.int32(0), jnp.int32(N_DP), add_replica, jnp.zeros((FF // 2, EXPERTS * D), jnp.float32))
    gradient = unpack_rows(summed, group_codes).astype(jnp.bfloat16)
    local_owner = owner.reshape(N_DP, BR_DEV, N_MP, BC_DEV).transpose(0, 2, 1, 3).reshape(N_DP, N_MP, NB_DEV)
    peer_index = jnp.arange(N_MP, dtype=jnp.int32)
    owner_hits = (local_owner[..., None] == peer_index).astype(jnp.int32)
    per_sender = lax.optimization_barrier(jnp.sum(owner_hits, axis=2))
    before_sender = jnp.cumsum(per_sender, axis=1) - per_sender
    before_local = jnp.cumsum(owner_hits, axis=2) - owner_hits
    slot_index = lax.optimization_barrier(jnp.sum(owner_hits * (before_sender[:, :, None, :] + before_local), axis=3))
    row_index = jnp.arange(N_DP, dtype=jnp.int32)[:, None, None]
    root_slot = ((row_index * N_MP + local_owner) * CAPO + slot_index).astype(jnp.int32)
    grad_blocks = gradient.reshape(N_DP, BR_DEV, BLOCK, N_MP, BC_DEV, BLOCK).transpose(0, 3, 1, 4, 2, 5)
    grad_blocks = grad_blocks.reshape(N_DP * N_MP * NB_DEV, BLOCK, BLOCK)

    def one_block(operands):
        grad_block, chosen = operands
        return precondition_one(grad_block, left_root[chosen], right_root[chosen])
    scaled = lax.map(one_block, (grad_blocks, root_slot.reshape(-1)))
    placed = scaled.reshape(N_DP, N_MP, BR_DEV, BC_DEV, BLOCK, BLOCK).transpose(0, 2, 4, 1, 3, 5)
    placed = placed.reshape(FF, EXPERTS * D)
    select_first, select_second = kept_selectors(group_codes)
    kept_mask = (select_first + select_second).reshape(FF, EXPERTS * D)
    return (placed.astype(jnp.float32) * kept_mask).astype(jnp.bfloat16)
```

```python
import functools

import jax
import jax.numpy as jnp
from jax import lax
from jax.experimental import pallas as pl
from jax.experimental.pallas import tpu as pltpu
from jax.sharding import PartitionSpec as P

BLOCK = 512
HALF = BLOCK // 2
LANES = 128
SIDE = 4
SLOT_ROWS = BLOCK * BLOCK // LANES + 16
MESH = pl.DeviceIdType.MESH

NEAR = [(1, 0), (0, 1), (3, 0), (0, 3)]
STRAIGHT = [(2, 0), (0, 2)]
DIAGONAL = [(1, 1), (3, 3), (1, 3), (3, 1)]
FAR = [(2, 2)]
RELAYED = [
    ((2, 1), (0, 1), (2, 0)),
    ((1, 2), (1, 0), (0, 2)),
    ((2, 3), (0, 3), (2, 0)),
    ((3, 2), (3, 0), (0, 2)),
]


def slot_of(displacement):
    return displacement[1] * SIDE + displacement[0]


def triangles():
    row = lax.broadcasted_iota(jnp.int32, (HALF, HALF), 0)
    column = lax.broadcasted_iota(jnp.int32, (HALF, HALF), 1)
    as_bf16 = lambda test: jnp.where(test, 1.0, 0.0).astype(jnp.bfloat16)
    return as_bf16(row >= column), as_bf16(row < column), as_bf16(row > column), as_bf16(row == column)


def exchange_kernel(
    tokens, rows, columns, dp_size, mp_size, capacity,
    targets_ref, left_hbm, right_hbm, hidden_hbm, grads_hbm,
    roots_out, hidden_out, grads_out,
    left, right, send_slots, relay_slots, lists, lists_smem, ranks,
    load_sem, list_send, list_recv, slot_send, slot_recv, hop_send, hop_recv,
    gather_send, gather_recv, own_sem,
):
    d, m = lax.axis_index("dp"), lax.axis_index("mp")
    x, y = lax.rem(m, SIDE), m // SIDE

    def at(displacement):
        return lax.rem(y + displacement[1], SIDE) * SIDE + lax.rem(x + displacement[0], SIDE)

    loads = [
        pltpu.make_async_copy(left_hbm, left, load_sem.at[0]),
        pltpu.make_async_copy(right_hbm, right, load_sem.at[1]),
    ]
    for load in loads:
        load.start()

    barrier = pltpu.get_barrier_semaphore()
    for step in range(1, mp_size):
        pl.semaphore_signal(barrier, inc=1, device_id=(d, lax.rem(m + step, mp_size)), device_id_type=MESH)
    for step in range(1, dp_size):
        pl.semaphore_signal(barrier, inc=1, device_id=(lax.rem(d + step, dp_size), m), device_id_type=MESH)
    pl.semaphore_wait(barrier, mp_size - 1 + dp_size - 1)

    list_copies = []
    for step in range(1, mp_size):
        copy = pltpu.make_async_remote_copy(
            src_ref=targets_ref, dst_ref=lists.at[m], send_sem=list_send.at[step], recv_sem=list_recv.at[step],
            device_id=(d, lax.rem(m + step, mp_size)), device_id_type=MESH,
        )
        copy.start()
        list_copies.append(copy)
    lists[m] = targets_ref[...]

    expert = m * columns // (columns * SIDE)
    gathers = []
    for step in range(1, dp_size):
        peer = lax.rem(d + step, dp_size)
        features = pl.ds(pl.multiple_of(peer * rows, rows), rows)
        for which, (source, sink) in enumerate((
            (hidden_hbm.at[expert, :, features], hidden_out.at[d]),
            (grads_hbm, grads_out.at[d]),
        )):
            copy = pltpu.make_async_remote_copy(
                src_ref=source, dst_ref=sink, send_sem=gather_send.at[which, step], recv_sem=gather_recv.at[which, step],
                device_id=(peer, m), device_id_type=MESH,
            )
            copy.start()
            gathers.append(copy)
    own_features = pl.ds(pl.multiple_of(d * rows, rows), rows)
    own_copies = [
        pltpu.make_async_copy(hidden_hbm.at[expert, :, own_features], hidden_out.at[d], own_sem.at[0]),
        pltpu.make_async_copy(grads_hbm, grads_out.at[d], own_sem.at[1]),
    ]
    for copy in own_copies:
        copy.start()

    for copy in list_copies:
        copy.wait()
    to_smem = pltpu.make_async_copy(lists, lists_smem, load_sem.at[2])
    to_smem.start()
    to_smem.wait()

    def rank_step(sender, taken):
        ranks[sender] = jnp.minimum(taken, capacity - 1)
        hit = jnp.int32(0)
        for j in range(6):
            hit = jnp.where(lists_smem[sender, 0, j] == m, jnp.int32(1), hit)
        return taken + hit

    lax.fori_loop(0, mp_size, rank_step, jnp.int32(0))
    for load in loads:
        load.wait()

    lower, upper, _, eye = triangles()

    def pack(displacement):
        slot = slot_of(displacement)
        rank = ranks[at(displacement)]
        place = lax.broadcasted_iota(jnp.int32, (16, LANES), 0)
        extra = jnp.zeros((16, LANES), jnp.float32)
        for q, root in enumerate((left, right)):
            a = root[rank, 0:HALF, 0:HALF]
            b = root[rank, 0:HALF, HALF:BLOCK]
            c = root[rank, HALF:BLOCK, HALF:BLOCK]
            mixed = a * lower + c * upper
            diagonal = jnp.sum((c * eye).astype(jnp.float32), axis=0, keepdims=True)
            base = q * 4 * HALF
            for half in range(2):
                lanes = slice(half * LANES, (half + 1) * LANES)
                send_slots[slot, base + half * HALF : base + (half + 1) * HALF, :] = b[:, lanes]
                send_slots[slot, base + (2 + half) * HALF : base + (3 + half) * HALF, :] = mixed[:, lanes]
                extra = jnp.where(place == 2 * q + half, diagonal[:, lanes], extra)
        send_slots[slot, SLOT_ROWS - 16 : SLOT_ROWS, :] = extra.astype(jnp.bfloat16)

    hops = []
    for k, (displacement, first, second) in enumerate(RELAYED):
        pack(displacement)
        copy = pltpu.make_async_remote_copy(
            src_ref=send_slots.at[slot_of(displacement)], dst_ref=relay_slots.at[k],
            send_sem=hop_send.at[k], recv_sem=hop_recv.at[k], device_id=(d, at(first)), device_id_type=MESH,
        )
        copy.start()
        hops.append(copy)
    sends = []
    for displacement in FAR + DIAGONAL + STRAIGHT + NEAR:
        pack(displacement)
        slot = slot_of(displacement)
        copy = pltpu.make_async_remote_copy(
            src_ref=send_slots.at[slot], dst_ref=roots_out.at[slot],
            send_sem=slot_send.at[slot], recv_sem=slot_recv.at[slot], device_id=(d, at(displacement)), device_id_type=MESH,
        )
        copy.start()
        sends.append(copy)
    pack((0, 0))
    own_slot = pltpu.make_async_copy(send_slots.at[0], roots_out.at[0], own_sem.at[2])
    own_slot.start()
    for k, (displacement, first, second) in enumerate(RELAYED):
        hops[k].wait_recv()
        slot = slot_of(displacement)
        copy = pltpu.make_async_remote_copy(
            src_ref=relay_slots.at[k], dst_ref=roots_out.at[slot],
            send_sem=slot_send.at[slot], recv_sem=slot_recv.at[slot], device_id=(d, at(second)), device_id_type=MESH,
        )
        copy.start()
        sends.append(copy)
    own_slot.wait()
    for copy in own_copies:
        copy.wait()
    for hop in hops:
        hop.wait_send()
    for copy in gathers + sends:
        copy.wait()


def unpack(slot, q, full):
    lower, upper, strict, eye = triangles()
    base = q * 4 * HALF
    b = jnp.concatenate([slot[base : base + HALF, :], slot[base + HALF : base + 2 * HALF, :]], axis=1)
    mixed = jnp.concatenate([slot[base + 2 * HALF : base + 3 * HALF, :], slot[base + 3 * HALF : base + 4 * HALF, :]], axis=1)
    extra = slot[SLOT_ROWS - 16 : SLOT_ROWS, :].astype(jnp.float32)
    diagonal = jnp.concatenate([extra[2 * q : 2 * q + 1, :], extra[2 * q + 1 : 2 * q + 2, :]], axis=1).astype(jnp.bfloat16)
    turned = mixed.T
    full[0:HALF, 0:HALF] = mixed * lower + turned * upper
    full[0:HALF, HALF:BLOCK] = b
    full[HALF:BLOCK, 0:HALF] = b.T
    full[HALF:BLOCK, HALF:BLOCK] = mixed * upper + turned * strict + eye * diagonal


KEPT_ROWS = sum(bits << (4 * code) for code, bits in enumerate((3, 5, 9, 6, 10, 12)))


def kept_rows(words):
    count, columns = words.shape
    spread = jnp.broadcast_to(words[:, None, :], (count, 16, columns)).reshape(count * 16, columns)
    row = lax.broadcasted_iota(jnp.int32, (count * 16, columns), 0)
    code = jnp.bitwise_and(lax.shift_right_logical(spread, jnp.bitwise_and(row, 15) // 4 * 3), 7)
    bits = lax.shift_right_logical(jnp.full_like(code, KEPT_ROWS), code * 4 + jnp.bitwise_and(row, 3))
    return jnp.bitwise_and(bits, 1) == 1


def block_kernel(places, slot_ref, hidden_ref, grads_ref, words_ref, out_ref, left, right):
    tokens = hidden_ref.shape[0] * hidden_ref.shape[1]
    gradient = lax.dot_general(
        hidden_ref[...].reshape(tokens, BLOCK), grads_ref[...].reshape(tokens, BLOCK),
        (((0,), (0,)), ((), ())), preferred_element_type=jnp.float32,
    )
    kept = kept_rows(words_ref[...])
    block = jnp.where(kept, gradient, 0.0).astype(jnp.bfloat16)
    unpack(slot_ref.at[0], 0, left)
    unpack(slot_ref.at[0], 1, right)
    right_applied = jnp.dot(block, right[...], preferred_element_type=jnp.float32).astype(jnp.bfloat16)
    preconditioned = jnp.dot(left[...], right_applied, preferred_element_type=jnp.float32)
    wide = block.astype(jnp.float32)
    count = BLOCK * BLOCK
    numerator = jnp.sqrt(jnp.sum(wide * wide) / count)
    denominator = jnp.sqrt(jnp.sum(preconditioned * preconditioned) / count + 1e-06)
    out_ref[...] = jnp.where(kept, preconditioned * (numerator / denominator), 0.0).astype(jnp.bfloat16)


def body(dp_size, mp_size, hidden, out_grads, mask_words, owner, left_root, right_root):
    tokens, columns = out_grads.shape
    rows = hidden.shape[2] // dp_size
    capacity = left_root.shape[0]
    d, m = lax.axis_index("dp"), lax.axis_index("mp")
    targets = owner.reshape(-1)
    block_count = targets.shape[0]
    tile = jnp.full((8, LANES), -1, jnp.int32).at[0, :block_count].set(targets)
    any_space = pl.BlockSpec(memory_space=pl.ANY)
    slots, all_hidden, all_grads = pl.pallas_call(
        functools.partial(exchange_kernel, tokens, rows, columns, dp_size, mp_size, capacity),
        out_shape=(
            jax.ShapeDtypeStruct((mp_size, SLOT_ROWS, LANES), jnp.bfloat16),
            jax.ShapeDtypeStruct((dp_size, tokens, rows), jnp.bfloat16),
            jax.ShapeDtypeStruct((dp_size, tokens, columns), jnp.bfloat16),
        ),
        in_specs=[pl.BlockSpec(memory_space=pltpu.VMEM)] + [any_space] * 4,
        out_specs=(any_space,) * 3,
        scratch_shapes=[
            pltpu.VMEM(left_root.shape, jnp.bfloat16),
            pltpu.VMEM(right_root.shape, jnp.bfloat16),
            pltpu.VMEM((mp_size, SLOT_ROWS, LANES), jnp.bfloat16),
            pltpu.VMEM((len(RELAYED), SLOT_ROWS, LANES), jnp.bfloat16),
            pltpu.VMEM((mp_size, 8, LANES), jnp.int32),
            pltpu.SMEM((mp_size, 8, LANES), jnp.int32),
            pltpu.SMEM((mp_size,), jnp.int32),
            pltpu.SemaphoreType.DMA((3,)),
            pltpu.SemaphoreType.DMA((mp_size,)),
            pltpu.SemaphoreType.DMA((mp_size,)),
            pltpu.SemaphoreType.DMA((mp_size,)),
            pltpu.SemaphoreType.DMA((mp_size,)),
            pltpu.SemaphoreType.DMA((len(RELAYED),)),
            pltpu.SemaphoreType.DMA((len(RELAYED),)),
            pltpu.SemaphoreType.DMA((2, dp_size)),
            pltpu.SemaphoreType.DMA((2, dp_size)),
            pltpu.SemaphoreType.DMA((3,)),
        ],
        compiler_params=pltpu.CompilerParams(
            collective_id=0, has_side_effects=True, vmem_limit_bytes=56 * 2**20
        ),
        name="exchange",
    )(tile, left_root, right_root, hidden, out_grads)

    away_x = (m % SIDE - targets % SIDE + SIDE) % SIDE
    away_y = (m // SIDE - targets // SIDE + SIDE) % SIDE
    places = jnp.concatenate([away_y * SIDE + away_x, d[None]]).astype(jnp.int32)
    across = columns // BLOCK
    return pl.pallas_call(
        block_kernel,
        out_shape=jax.ShapeDtypeStruct((rows, columns), jnp.bfloat16),
        grid_spec=pltpu.PrefetchScalarGridSpec(
            num_scalar_prefetch=1,
            grid=(block_count,),
            in_specs=[
                pl.BlockSpec((1, SLOT_ROWS, LANES), lambda j, places: (places[j], 0, 0)),
                pl.BlockSpec((dp_size, tokens, BLOCK), lambda j, places: (0, 0, j // across)),
                pl.BlockSpec((dp_size, tokens, BLOCK), lambda j, places: (0, 0, j % across)),
                pl.BlockSpec(
                    (BLOCK // 16, BLOCK),
                    lambda j, places: (places[block_count] * (rows // BLOCK) + j // across, j % across),
                ),
            ],
            out_specs=pl.BlockSpec((BLOCK, BLOCK), lambda j, places: (j // across, j % across)),
            scratch_shapes=[
                pltpu.VMEM((BLOCK, BLOCK), jnp.bfloat16),
                pltpu.VMEM((BLOCK, BLOCK), jnp.bfloat16),
            ],
        ),
        compiler_params=pltpu.CompilerParams(vmem_limit_bytes=48 * 2**20),
        name="precondition",
    )(places, slots, all_hidden, all_grads, mask_words)


def solution(mesh):
    in_specs = (
        P(None, "dp", None),
        P("dp", "mp"),
        P(None, "mp"),
        P("dp", "mp"),
        P(("dp", "mp"), None, None),
        P(("dp", "mp"), None, None),
    )
    return jax.shard_map(
        functools.partial(body, mesh.shape["dp"], mesh.shape["mp"]),
        mesh=mesh, in_specs=in_specs, out_specs=P("dp", "mp"), check_vma=False,
    )
```

```python
import functools

import jax
import jax.numpy as jnp
from jax import lax
from jax.experimental import pallas as pl
from jax.experimental.pallas import tpu as pltpu
from jax.sharding import PartitionSpec as P

BLOCK = 512
HALF = BLOCK // 2
LANES = 128
SIDE = 4
SLOT_ROWS = BLOCK * BLOCK // LANES + 16
MESH = pl.DeviceIdType.MESH

NEAR = [(1, 0), (0, 1), (3, 0), (0, 3)]
STRAIGHT = [(2, 0), (0, 2)]
DIAGONAL = [(1, 1), (3, 3), (1, 3), (3, 1)]
FAR = [(2, 2)]
RELAYED = [
    ((2, 1), (0, 1), (2, 0)),
    ((1, 2), (1, 0), (0, 2)),
    ((2, 3), (0, 3), (2, 0)),
    ((3, 2), (3, 0), (0, 2)),
]
ORDER = [(0, 0)] + FAR + STRAIGHT + DIAGONAL + NEAR + [legs[0] for legs in RELAYED]
SLOT = {displacement: slot for slot, displacement in enumerate(ORDER)}

KEPT_ROWS = sum(bits << (4 * code) for code, bits in enumerate((3, 5, 9, 6, 10, 12)))


def kept_rows(words):
    count, columns = words.shape
    spread = jnp.broadcast_to(words[:, None, :], (count, 16, columns)).reshape(count * 16, columns)
    row = lax.broadcasted_iota(jnp.int32, (count * 16, columns), 0)
    code = jnp.bitwise_and(lax.shift_right_logical(spread, jnp.bitwise_and(row, 15) // 4 * 3), 7)
    bits = lax.shift_right_logical(jnp.full_like(code, KEPT_ROWS), code * 4 + jnp.bitwise_and(row, 3))
    return jnp.bitwise_and(bits, 1) == 1


def exchange_kernel(
    rows, columns, dp_size, mp_size,
    owner, left_hbm, right_hbm, hidden_hbm, grads_hbm, words_hbm,
    scaled_out,
    left, right, send_slots, relay_slots, slots, hidden, grads, words, blocks, kept, left_full, right_full, triangles,
    tile, lists, lists_smem, ranks, block_of_slot, norms,
    load_sem, list_send, list_recv, slot_send, slot_recv, hop_send, hop_recv, gather_send, gather_recv, out_sem,
):
    capacity = left.shape[0]
    down, across = owner.shape
    block_count = down * across
    d, m = lax.axis_index("dp"), lax.axis_index("mp")
    x, y = lax.rem(m, SIDE), m // SIDE

    def at(displacement):
        return lax.rem(y + displacement[1], SIDE) * SIDE + lax.rem(x + displacement[0], SIDE)

    expert = m * columns // (columns * SIDE)
    own_features = pl.ds(pl.multiple_of(d * rows, rows), rows)
    own_words = pl.ds(pl.multiple_of(d * (rows // 16), rows // 16), rows // 16)
    root_loads = [
        pltpu.make_async_copy(left_hbm, left, load_sem.at[0]),
        pltpu.make_async_copy(right_hbm, right, load_sem.at[1]),
    ]
    own_loads = [
        pltpu.make_async_copy(hidden_hbm.at[expert, :, own_features], hidden.at[d], load_sem.at[2]),
        pltpu.make_async_copy(grads_hbm, grads.at[d], load_sem.at[3]),
        pltpu.make_async_copy(words_hbm.at[own_words], words, load_sem.at[4]),
    ]
    for load in root_loads + own_loads:
        load.start()

    barrier = pltpu.get_barrier_semaphore()
    for step in range(1, mp_size):
        pl.semaphore_signal(barrier, inc=1, device_id=(d, lax.rem(m + step, mp_size)), device_id_type=MESH)
    for step in range(1, dp_size):
        pl.semaphore_signal(barrier, inc=1, device_id=(lax.rem(d + step, dp_size), m), device_id_type=MESH)

    targets = [owner[j // across, j % across] for j in range(block_count)]
    lane = lax.broadcasted_iota(jnp.int32, (8, LANES), 1)
    listed = jnp.full((8, LANES), -1, jnp.int32)
    for j in range(block_count):
        listed = jnp.where(lane == j, targets[j], listed)
    tile[...] = listed
    row = lax.broadcasted_iota(jnp.int32, (HALF, HALF), 0)
    column = lax.broadcasted_iota(jnp.int32, (HALF, HALF), 1)
    for k, test in enumerate((row >= column, row < column, row > column, row == column)):
        triangles[k] = jnp.where(test, 1.0, 0.0).astype(jnp.bfloat16)
    pl.semaphore_wait(barrier, mp_size - 1 + dp_size - 1)

    list_copies = []
    for step in range(1, mp_size):
        copy = pltpu.make_async_remote_copy(
            src_ref=tile, dst_ref=lists.at[m], send_sem=list_send.at[step], recv_sem=list_recv.at[step],
            device_id=(d, lax.rem(m + step, mp_size)), device_id_type=MESH,
        )
        copy.start()
        list_copies.append(copy)
    lists[m] = listed

    gathers = []
    for step in range(1, dp_size):
        peer = lax.rem(d + step, dp_size)
        features = pl.ds(pl.multiple_of(peer * rows, rows), rows)
        for which, (source, sink) in enumerate((
            (hidden_hbm.at[expert, :, features], hidden.at[d]),
            (grads_hbm, grads.at[d]),
        )):
            copy = pltpu.make_async_remote_copy(
                src_ref=source, dst_ref=sink, send_sem=gather_send.at[which, step], recv_sem=gather_recv.at[which, step],
                device_id=(peer, m), device_id_type=MESH,
            )
            copy.start()
            gathers.append(copy)

    for copy in list_copies:
        copy.wait()
    to_smem = pltpu.make_async_copy(lists, lists_smem, load_sem.at[5])
    to_smem.start()

    for slot, displacement in enumerate(ORDER):
        sender = at((SIDE - displacement[0], SIDE - displacement[1]))
        block = jnp.int32(0)
        for j in range(1, block_count):
            block = jnp.where(targets[j] == sender, jnp.int32(j), block)
        block_of_slot[slot] = block
    to_smem.wait()

    def rank_step(sender, taken):
        ranks[sender] = jnp.minimum(taken, capacity - 1)
        hit = jnp.int32(0)
        for j in range(block_count):
            hit = jnp.where(lists_smem[sender, 0, j] == m, jnp.int32(1), hit)
        return taken + hit

    lax.fori_loop(0, mp_size, rank_step, jnp.int32(0))
    for load in root_loads:
        load.wait()

    def pack(displacement):
        slot = SLOT[displacement]
        rank = ranks[at(displacement)]
        place = lax.broadcasted_iota(jnp.int32, (16, LANES), 0)
        extra = jnp.zeros((16, LANES), jnp.float32)
        for q, root in enumerate((left, right)):
            a = root[rank, 0:HALF, 0:HALF]
            b = root[rank, 0:HALF, HALF:BLOCK]
            c = root[rank, HALF:BLOCK, HALF:BLOCK]
            mixed = a * triangles[0] + c * triangles[1]
            diagonal = jnp.sum((c * triangles[3]).astype(jnp.float32), axis=0, keepdims=True)
            base = q * 4 * HALF
            for half in range(2):
                lanes = slice(half * LANES, (half + 1) * LANES)
                send_slots[slot, base + half * HALF : base + (half + 1) * HALF, :] = b[:, lanes]
                send_slots[slot, base + (2 + half) * HALF : base + (3 + half) * HALF, :] = mixed[:, lanes]
                extra = jnp.where(place == 2 * q + half, diagonal[:, lanes], extra)
        send_slots[slot, SLOT_ROWS - 16 : SLOT_ROWS, :] = extra.astype(jnp.bfloat16)

    hops = []
    for k, (displacement, first, second) in enumerate(RELAYED):
        pack(displacement)
        copy = pltpu.make_async_remote_copy(
            src_ref=send_slots.at[SLOT[displacement]], dst_ref=relay_slots.at[k],
            send_sem=hop_send.at[k], recv_sem=hop_recv.at[k], device_id=(d, at(first)), device_id_type=MESH,
        )
        copy.start()
        hops.append(copy)
    sends = []
    for displacement in FAR + DIAGONAL + STRAIGHT + NEAR:
        pack(displacement)
        slot = SLOT[displacement]
        copy = pltpu.make_async_remote_copy(
            src_ref=send_slots.at[slot], dst_ref=slots.at[slot],
            send_sem=slot_send.at[slot], recv_sem=slot_recv.at[slot], device_id=(d, at(displacement)), device_id_type=MESH,
        )
        copy.start()
        sends.append(copy)
    pack((0, 0))
    pltpu.make_async_copy(send_slots.at[0], slots.at[0], slot_recv.at[0]).start()
    for k, (displacement, first, second) in enumerate(RELAYED):
        hops[k].wait_recv()
        slot = SLOT[displacement]
        copy = pltpu.make_async_remote_copy(
            src_ref=relay_slots.at[k], dst_ref=slots.at[slot],
            send_sem=slot_send.at[slot], recv_sem=slot_recv.at[slot], device_id=(d, at(second)), device_id_type=MESH,
        )
        copy.start()
        sends.append(copy)

    for load in own_loads:
        load.wait()
    for copy in gathers:
        copy.wait()

    def gradient_step(j, carry):
        features = pl.ds(pl.multiple_of(j // across * BLOCK, BLOCK), BLOCK)
        places = pl.ds(pl.multiple_of(lax.rem(j, across) * BLOCK, BLOCK), BLOCK)
        gradient = lax.dot_general(
            hidden[:, :, features].reshape(-1, BLOCK), grads[:, :, places].reshape(-1, BLOCK),
            (((0,), (0,)), ((), ())), preferred_element_type=jnp.float32,
        )
        in_words = pl.ds(pl.multiple_of(j // across * (BLOCK // 16), BLOCK // 16), BLOCK // 16)
        keep = jnp.where(kept_rows(words[in_words, places]), 1.0, 0.0)
        kept[j] = keep.astype(jnp.bfloat16)
        block = (gradient * keep).astype(jnp.bfloat16)
        blocks[j] = block
        wide = block.astype(jnp.float32)
        norms[j] = jnp.sum(wide * wide)
        return carry

    lax.fori_loop(0, block_count, gradient_step, 0)

    def unpack(slot, q, full):
        base = q * 4 * HALF
        part = lambda k: slots[slot, base + k * HALF : base + (k + 1) * HALF, :]
        b = jnp.concatenate([part(0), part(1)], axis=1)
        mixed = jnp.concatenate([part(2), part(3)], axis=1)
        extra = slots[slot, SLOT_ROWS - 16 : SLOT_ROWS, :].astype(jnp.float32)
        diagonal = jnp.concatenate([extra[2 * q : 2 * q + 1, :], extra[2 * q + 1 : 2 * q + 2, :]], axis=1)
        turned = mixed.T
        full[0:HALF, 0:HALF] = mixed * triangles[0] + turned * triangles[1]
        full[0:HALF, HALF:BLOCK] = b
        full[HALF:BLOCK, 0:HALF] = b.T
        full[HALF:BLOCK, HALF:BLOCK] = (
            mixed * triangles[1] + turned * triangles[2] + triangles[3] * diagonal.astype(jnp.bfloat16)
        )

    def out_copy(slot):
        return pltpu.make_async_copy(slots.at[slot, pl.ds(0, 4 * BLOCK)], scaled_out.at[slot], out_sem.at[slot])

    def slot_step(slot, carry):
        pltpu.make_async_copy(send_slots.at[slot], slots.at[slot], slot_recv.at[slot]).wait()
        j = block_of_slot[slot]
        unpack(slot, 1, right_full)
        right_applied = jnp.dot(blocks[j], right_full[...], preferred_element_type=jnp.float32).astype(jnp.bfloat16)
        unpack(slot, 0, left_full)
        preconditioned = jnp.dot(left_full[...], right_applied, preferred_element_type=jnp.float32)
        count = BLOCK * BLOCK
        numerator = jnp.sqrt(norms[j] / count)
        denominator = jnp.sqrt(jnp.sum(preconditioned * preconditioned) / count + 1e-06)
        scaled = (preconditioned * (numerator / denominator)).astype(jnp.bfloat16) * kept[j]
        for k in range(BLOCK // LANES):
            slots[slot, k * BLOCK : (k + 1) * BLOCK, :] = scaled[:, k * LANES : (k + 1) * LANES]
        out_copy(slot).start()
        return carry

    lax.fori_loop(0, mp_size, slot_step, 0)
    for hop in hops:
        hop.wait_send()
    for send in sends:
        send.wait_send()
    for slot in range(mp_size):
        out_copy(slot).wait()


def place_kernel(owner, scaled, out, held, load_sem, store_sem):
    down, across = owner.shape
    m = lax.axis_index("mp")
    loads, stores = [], []
    for j in range(down * across):
        target = owner[j // across, j % across]
        away_x = lax.rem(lax.rem(m, SIDE) - lax.rem(target, SIDE) + SIDE, SIDE)
        away_y = lax.rem(m // SIDE - target // SIDE + SIDE, SIDE)
        slot = jnp.int32(0)
        for index, (dx, dy) in enumerate(ORDER):
            slot = jnp.where((away_x == dx) & (away_y == dy), jnp.int32(index), slot)
        rows = pl.ds(j // across * BLOCK, BLOCK)
        columns = pl.ds(j % across * BLOCK, BLOCK)
        loads.append([
            pltpu.make_async_copy(
                scaled.at[slot, pl.ds(k * BLOCK, BLOCK)], held.at[j, :, pl.ds(k * LANES, LANES)], load_sem.at[j, k]
            )
            for k in range(BLOCK // LANES)
        ])
        stores.append(pltpu.make_async_copy(held.at[j], out.at[rows, columns], store_sem.at[j]))
        for load in loads[-1]:
            load.start()
    for parts, store in zip(loads, stores):
        for load in parts:
            load.wait()
        store.start()
    for store in stores:
        store.wait()


def body(dp_size, mp_size, hidden, out_grads, mask_words, owner, left_root, right_root):
    tokens, columns = out_grads.shape
    rows = hidden.shape[2] // dp_size
    block_count = owner.size
    any_space = pl.BlockSpec(memory_space=pl.ANY)
    in_smem = pl.BlockSpec(memory_space=pltpu.SMEM)
    blocks = pltpu.VMEM((block_count, BLOCK, BLOCK), jnp.bfloat16)
    slots = pltpu.VMEM((mp_size, SLOT_ROWS, LANES), jnp.bfloat16)
    full = pltpu.VMEM((BLOCK, BLOCK), jnp.bfloat16)
    scaled = pl.pallas_call(
        functools.partial(exchange_kernel, rows, columns, dp_size, mp_size),
        out_shape=jax.ShapeDtypeStruct((mp_size, 4 * BLOCK, LANES), jnp.bfloat16),
        in_specs=[in_smem] + [any_space] * 5,
        out_specs=any_space,
        scratch_shapes=[
            pltpu.VMEM(left_root.shape, jnp.bfloat16),
            pltpu.VMEM(right_root.shape, jnp.bfloat16),
            slots,
            pltpu.VMEM((len(RELAYED), SLOT_ROWS, LANES), jnp.bfloat16),
            slots,
            pltpu.VMEM((dp_size, tokens, rows), jnp.bfloat16),
            pltpu.VMEM((dp_size, tokens, columns), jnp.bfloat16),
            pltpu.VMEM((rows // 16, columns), jnp.int32),
            blocks,
            blocks,
            full,
            full,
            pltpu.VMEM((4, HALF, HALF), jnp.bfloat16),
            pltpu.VMEM((8, LANES), jnp.int32),
            pltpu.VMEM((mp_size, 8, LANES), jnp.int32),
            pltpu.SMEM((mp_size, 8, LANES), jnp.int32),
            pltpu.SMEM((mp_size,), jnp.int32),
            pltpu.SMEM((mp_size,), jnp.int32),
            pltpu.SMEM((block_count,), jnp.float32),
            pltpu.SemaphoreType.DMA((6,)),
            pltpu.SemaphoreType.DMA((mp_size,)),
            pltpu.SemaphoreType.DMA((mp_size,)),
            pltpu.SemaphoreType.DMA((mp_size,)),
            pltpu.SemaphoreType.DMA((mp_size,)),
            pltpu.SemaphoreType.DMA((len(RELAYED),)),
            pltpu.SemaphoreType.DMA((len(RELAYED),)),
            pltpu.SemaphoreType.DMA((2, dp_size)),
            pltpu.SemaphoreType.DMA((2, dp_size)),
            pltpu.SemaphoreType.DMA((mp_size,)),
        ],
        compiler_params=pltpu.CompilerParams(
            collective_id=0, has_side_effects=True, vmem_limit_bytes=58 * 2**20
        ),
        name="exchange",
    )(owner, left_root, right_root, hidden, out_grads, mask_words)
    return pl.pallas_call(
        place_kernel,
        out_shape=jax.ShapeDtypeStruct((rows, columns), jnp.bfloat16),
        in_specs=[in_smem, any_space],
        out_specs=any_space,
        scratch_shapes=[
            blocks,
            pltpu.SemaphoreType.DMA((block_count, BLOCK // LANES)),
            pltpu.SemaphoreType.DMA((block_count,)),
        ],
        name="place",
    )(owner, scaled)


def solution(mesh):
    in_specs = (
        P(None, "dp", None),
        P("dp", "mp"),
        P(None, "mp"),
        P("dp", "mp"),
        P(("dp", "mp"), None, None),
        P(("dp", "mp"), None, None),
    )
    return jax.shard_map(
        functools.partial(body, mesh.shape["dp"], mesh.shape["mp"]),
        mesh=mesh, in_specs=in_specs, out_specs=P("dp", "mp"), check_vma=False,
    )
```

```python
import functools

import jax
import jax.numpy as jnp
from jax import lax
from jax.experimental import pallas as pl
from jax.experimental.pallas import tpu as pltpu
from jax.sharding import PartitionSpec as P

BLOCK = 512
HALF = BLOCK // 2
LANES = 128
SIDE = 4
SLOT_ROWS = BLOCK * BLOCK // LANES + 16
MESH = pl.DeviceIdType.MESH

NEAR = [(1, 0), (0, 1), (3, 0), (0, 3)]
STRAIGHT = [(2, 0), (0, 2)]
DIAGONAL = [(1, 1), (3, 3), (1, 3), (3, 1)]
FAR = [(2, 2)]
RELAYED = [
    ((2, 1), (0, 1), (2, 0)),
    ((1, 2), (1, 0), (0, 2)),
    ((2, 3), (0, 3), (2, 0)),
    ((3, 2), (3, 0), (0, 2)),
]
ORDER = [(0, 0)] + NEAR + STRAIGHT + DIAGONAL + FAR + [legs[0] for legs in RELAYED]
DIRECT = len(ORDER) - len(RELAYED)
SLOT = {displacement: slot for slot, displacement in enumerate(ORDER)}

KEPT_ROWS = sum(bits << (4 * code) for code, bits in enumerate((3, 5, 9, 6, 10, 12)))


def kept_rows(words):
    count, columns = words.shape
    spread = jnp.broadcast_to(words[:, None, :], (count, 16, columns)).reshape(count * 16, columns)
    row = lax.broadcasted_iota(jnp.int32, (count * 16, columns), 0)
    code = jnp.bitwise_and(lax.shift_right_logical(spread, jnp.bitwise_and(row, 15) // 4 * 3), 7)
    bits = lax.shift_right_logical(jnp.full_like(code, KEPT_ROWS), code * 4 + jnp.bitwise_and(row, 3))
    return jnp.bitwise_and(bits, 1) == 1


def exchange_kernel(
    rows, columns, dp_size, mp_size,
    owner, left_hbm, right_hbm, hidden_hbm, grads_hbm, words_hbm,
    scaled_out,
    left, right, send_slots, relay_slots, slots, hidden, grads, words, blocks, kept, left_full, right_full, triangles, halfway,
    tile, lists, lists_smem, ranks, block_of_slot, norms,
    load_sem, list_send, list_recv, slot_send, slot_recv, hop_send, hop_recv, last_send, last_recv, gather_send, gather_recv, out_sem,
):
    capacity = left.shape[0]
    down, across = owner.shape
    block_count = down * across
    d, m = lax.axis_index("dp"), lax.axis_index("mp")
    x, y = lax.rem(m, SIDE), m // SIDE

    def at(displacement):
        return lax.rem(y + displacement[1], SIDE) * SIDE + lax.rem(x + displacement[0], SIDE)

    expert = m * columns // (columns * SIDE)
    own_features = pl.ds(pl.multiple_of(d * rows, rows), rows)
    own_words = pl.ds(pl.multiple_of(d * (rows // 16), rows // 16), rows // 16)
    root_loads = [
        pltpu.make_async_copy(left_hbm, left, load_sem.at[0]),
        pltpu.make_async_copy(right_hbm, right, load_sem.at[1]),
    ]
    own_loads = [
        pltpu.make_async_copy(hidden_hbm.at[expert, :, own_features], hidden.at[d], load_sem.at[2]),
        pltpu.make_async_copy(grads_hbm, grads.at[d], load_sem.at[3]),
        pltpu.make_async_copy(words_hbm.at[own_words], words, load_sem.at[4]),
    ]
    for load in root_loads + own_loads:
        load.start()

    barrier = pltpu.get_barrier_semaphore()
    for step in range(1, mp_size):
        pl.semaphore_signal(barrier, inc=1, device_id=(d, lax.rem(m + step, mp_size)), device_id_type=MESH)
    for step in range(1, dp_size):
        pl.semaphore_signal(barrier, inc=1, device_id=(lax.rem(d + step, dp_size), m), device_id_type=MESH)

    targets = [owner[j // across, j % across] for j in range(block_count)]
    lane = lax.broadcasted_iota(jnp.int32, (1, LANES), 1)
    listed = jnp.full((1, LANES), -1, jnp.int32)
    for j in range(block_count):
        listed = jnp.where(lane == j, targets[j], listed)
    tile[...] = listed
    row = lax.broadcasted_iota(jnp.int32, (HALF, HALF), 0)
    column = lax.broadcasted_iota(jnp.int32, (HALF, HALF), 1)
    for k, test in enumerate((row >= column, row < column, row > column, row == column)):
        triangles[k] = jnp.where(test, 1.0, 0.0).astype(jnp.bfloat16)
    pl.semaphore_wait(barrier, mp_size - 1 + dp_size - 1)

    for step in range(1, mp_size):
        pltpu.make_async_remote_copy(
            src_ref=tile, dst_ref=lists.at[m], send_sem=list_send.at[0], recv_sem=list_recv.at[0],
            device_id=(d, lax.rem(m + step, mp_size)), device_id_type=MESH,
        ).start()
    lists[m] = listed

    gathers = []
    for step in range(1, dp_size):
        peer = lax.rem(d + step, dp_size)
        features = pl.ds(pl.multiple_of(peer * rows, rows), rows)
        for which, (source, sink) in enumerate((
            (hidden_hbm.at[expert, :, features], hidden.at[d]),
            (grads_hbm, grads.at[d]),
        )):
            copy = pltpu.make_async_remote_copy(
                src_ref=source, dst_ref=sink, send_sem=gather_send.at[which, step], recv_sem=gather_recv.at[which, step],
                device_id=(peer, m), device_id_type=MESH,
            )
            copy.start()
            gathers.append(copy)

    others = lists.at[pl.ds(0, mp_size - 1)]
    pltpu.make_async_copy(others, others, list_recv.at[0]).wait()
    to_smem = pltpu.make_async_copy(lists, lists_smem, load_sem.at[5])
    to_smem.start()

    for slot, displacement in enumerate(ORDER):
        sender = at((SIDE - displacement[0], SIDE - displacement[1]))
        block = jnp.int32(0)
        for j in range(1, block_count):
            block = jnp.where(targets[j] == sender, jnp.int32(j), block)
        block_of_slot[slot] = block
    to_smem.wait()

    def rank_step(sender, taken):
        ranks[sender] = jnp.minimum(taken, capacity - 1)
        hit = jnp.int32(0)
        for j in range(block_count):
            hit = jnp.where(lists_smem[sender, 0, j] == m, jnp.int32(1), hit)
        return taken + hit

    lax.fori_loop(0, mp_size, rank_step, jnp.int32(0))
    for load in root_loads:
        load.wait()

    def pack(displacement):
        slot = SLOT[displacement]
        rank = ranks[at(displacement)]
        place = lax.broadcasted_iota(jnp.int32, (16, LANES), 0)
        extra = jnp.zeros((16, LANES), jnp.float32)
        for q, root in enumerate((left, right)):
            a = root[rank, 0:HALF, 0:HALF]
            b = root[rank, 0:HALF, HALF:BLOCK]
            c = root[rank, HALF:BLOCK, HALF:BLOCK]
            mixed = a * triangles[0] + c * triangles[1]
            diagonal = jnp.sum((c * triangles[3]).astype(jnp.float32), axis=0, keepdims=True)
            base = q * 4 * HALF
            for half in range(2):
                lanes = slice(half * LANES, (half + 1) * LANES)
                send_slots[slot, base + half * HALF : base + (half + 1) * HALF, :] = b[:, lanes]
                send_slots[slot, base + (2 + half) * HALF : base + (3 + half) * HALF, :] = mixed[:, lanes]
                extra = jnp.where(place == 2 * q + half, diagonal[:, lanes], extra)
        send_slots[slot, SLOT_ROWS - 16 : SLOT_ROWS, :] = extra.astype(jnp.bfloat16)

    parts = [pl.ds(BLOCK * HALF // LANES, SLOT_ROWS - BLOCK * HALF // LANES), pl.ds(0, BLOCK * HALF // LANES)]
    hops = [[], []]
    for k, (displacement, first, second) in enumerate(RELAYED):
        pack(displacement)
        for p, part in enumerate(parts):
            copy = pltpu.make_async_remote_copy(
                src_ref=send_slots.at[SLOT[displacement], part], dst_ref=relay_slots.at[k, part],
                send_sem=hop_send.at[p, k], recv_sem=hop_recv.at[p, k], device_id=(d, at(first)), device_id_type=MESH,
            )
            copy.start()
            hops[p].append(copy)
    sends = []
    for displacement in NEAR + STRAIGHT + DIAGONAL + FAR:
        pack(displacement)
        slot = SLOT[displacement]
        copy = pltpu.make_async_remote_copy(
            src_ref=send_slots.at[slot], dst_ref=slots.at[slot],
            send_sem=slot_send.at[slot], recv_sem=slot_recv.at[slot], device_id=(d, at(displacement)), device_id_type=MESH,
        )
        copy.start()
        sends.append(copy)
    pack((0, 0))
    pltpu.make_async_copy(send_slots.at[0], slots.at[0], slot_recv.at[0]).start()
    for p, part in enumerate(parts):
        for k, (displacement, first, second) in enumerate(RELAYED):
            hops[p][k].wait_recv()
            slot = SLOT[displacement]
            copy = pltpu.make_async_remote_copy(
                src_ref=relay_slots.at[k, part], dst_ref=slots.at[slot, part],
                send_sem=last_send.at[p, k], recv_sem=last_recv.at[p, k], device_id=(d, at(second)), device_id_type=MESH,
            )
            copy.start()
            sends.append(copy)

    for load in own_loads:
        load.wait()
    for copy in gathers:
        copy.wait()

    def gradient_step(j, carry):
        features = pl.ds(pl.multiple_of(j // across * BLOCK, BLOCK), BLOCK)
        places = pl.ds(pl.multiple_of(lax.rem(j, across) * BLOCK, BLOCK), BLOCK)
        gradient = lax.dot_general(
            hidden[:, :, features].reshape(-1, BLOCK), grads[:, :, places].reshape(-1, BLOCK),
            (((0,), (0,)), ((), ())), preferred_element_type=jnp.float32,
        )
        in_words = pl.ds(pl.multiple_of(j // across * (BLOCK // 16), BLOCK // 16), BLOCK // 16)
        keep = jnp.where(kept_rows(words[in_words, places]), 1.0, 0.0)
        kept[j] = keep.astype(jnp.bfloat16)
        block = (gradient * keep).astype(jnp.bfloat16)
        blocks[j] = block
        wide = block.astype(jnp.float32)
        norms[j] = jnp.sum(wide * wide)
        return carry

    lax.fori_loop(0, block_count, gradient_step, 0)

    def unpack(slot, q, full):
        base = q * 4 * HALF
        part = lambda k: slots[slot, base + k * HALF : base + (k + 1) * HALF, :]
        b = jnp.concatenate([part(0), part(1)], axis=1)
        mixed = jnp.concatenate([part(2), part(3)], axis=1)
        extra = slots[slot, SLOT_ROWS - 16 : SLOT_ROWS, :].astype(jnp.float32)
        diagonal = jnp.concatenate([extra[2 * q : 2 * q + 1, :], extra[2 * q + 1 : 2 * q + 2, :]], axis=1)
        turned = mixed.T
        full[0:HALF, 0:HALF] = mixed * triangles[0] + turned * triangles[1]
        full[0:HALF, HALF:BLOCK] = b
        full[HALF:BLOCK, 0:HALF] = b.T
        full[HALF:BLOCK, HALF:BLOCK] = (
            mixed * triangles[1] + turned * triangles[2] + triangles[3] * diagonal.astype(jnp.bfloat16)
        )

    def out_copy(slot):
        return pltpu.make_async_copy(slots.at[slot, pl.ds(0, 4 * BLOCK)], scaled_out.at[slot], out_sem.at[slot])

    def apply_right(slot):
        unpack(slot, 1, right_full)
        block = blocks[block_of_slot[slot]]
        return jnp.dot(block, right_full[...], preferred_element_type=jnp.float32).astype(jnp.bfloat16)

    def finish(slot, right_applied):
        j = block_of_slot[slot]
        unpack(slot, 0, left_full)
        preconditioned = jnp.dot(left_full[...], right_applied, preferred_element_type=jnp.float32)
        count = BLOCK * BLOCK
        numerator = jnp.sqrt(norms[j] / count)
        denominator = jnp.sqrt(jnp.sum(preconditioned * preconditioned) / count + 1e-06)
        scaled = (preconditioned * (numerator / denominator)).astype(jnp.bfloat16) * kept[j]
        for k in range(BLOCK // LANES):
            slots[slot, k * BLOCK : (k + 1) * BLOCK, :] = scaled[:, k * LANES : (k + 1) * LANES]
        out_copy(slot).start()

    def direct_step(slot, carry):
        pltpu.make_async_copy(send_slots.at[slot], slots.at[slot], slot_recv.at[slot]).wait()
        finish(slot, apply_right(slot))
        return carry

    def right_step(k, carry):
        part = parts[0]
        pltpu.make_async_copy(send_slots.at[k, part], relay_slots.at[k, part], last_recv.at[0, k]).wait()
        halfway[k] = apply_right(k + DIRECT)
        return carry

    def left_step(k, carry):
        part = parts[1]
        pltpu.make_async_copy(send_slots.at[k, part], relay_slots.at[k, part], last_recv.at[1, k]).wait()
        finish(k + DIRECT, halfway[k])
        return carry

    lax.fori_loop(0, DIRECT, direct_step, 0)
    lax.fori_loop(0, len(RELAYED), right_step, 0)
    lax.fori_loop(0, len(RELAYED), left_step, 0)
    pltpu.make_async_copy(others, others, list_send.at[0]).wait()
    for hop in hops[0] + hops[1]:
        hop.wait_send()
    for send in sends:
        send.wait_send()
    for slot in range(mp_size):
        out_copy(slot).wait()


def place_kernel(owner, scaled, out, held, load_sem, store_sem):
    down, across = owner.shape
    m = lax.axis_index("mp")
    loads, stores = [], []
    for j in range(down * across):
        target = owner[j // across, j % across]
        away_x = lax.rem(lax.rem(m, SIDE) - lax.rem(target, SIDE) + SIDE, SIDE)
        away_y = lax.rem(m // SIDE - target // SIDE + SIDE, SIDE)
        slot = jnp.int32(0)
        for index, (dx, dy) in enumerate(ORDER):
            slot = jnp.where((away_x == dx) & (away_y == dy), jnp.int32(index), slot)
        rows = pl.ds(j // across * BLOCK, BLOCK)
        columns = pl.ds(j % across * BLOCK, BLOCK)
        loads.append([
            pltpu.make_async_copy(
                scaled.at[slot, pl.ds(k * BLOCK, BLOCK)], held.at[j, :, pl.ds(k * LANES, LANES)], load_sem.at[j, k]
            )
            for k in range(BLOCK // LANES)
        ])
        stores.append(pltpu.make_async_copy(held.at[j], out.at[rows, columns], store_sem.at[j]))
        for load in loads[-1]:
            load.start()
    for parts, store in zip(loads, stores):
        for load in parts:
            load.wait()
        store.start()
    for store in stores:
        store.wait()


def body(dp_size, mp_size, hidden, out_grads, mask_words, owner, left_root, right_root):
    tokens, columns = out_grads.shape
    rows = hidden.shape[2] // dp_size
    block_count = owner.size
    any_space = pl.BlockSpec(memory_space=pl.ANY)
    in_smem = pl.BlockSpec(memory_space=pltpu.SMEM)
    blocks = pltpu.VMEM((block_count, BLOCK, BLOCK), jnp.bfloat16)
    slots = pltpu.VMEM((mp_size, SLOT_ROWS, LANES), jnp.bfloat16)
    full = pltpu.VMEM((BLOCK, BLOCK), jnp.bfloat16)
    scaled = pl.pallas_call(
        functools.partial(exchange_kernel, rows, columns, dp_size, mp_size),
        out_shape=jax.ShapeDtypeStruct((mp_size, 4 * BLOCK, LANES), jnp.bfloat16),
        in_specs=[in_smem] + [any_space] * 5,
        out_specs=any_space,
        scratch_shapes=[
            pltpu.VMEM(left_root.shape, jnp.bfloat16),
            pltpu.VMEM(right_root.shape, jnp.bfloat16),
            slots,
            pltpu.VMEM((len(RELAYED), SLOT_ROWS, LANES), jnp.bfloat16),
            slots,
            pltpu.VMEM((dp_size, tokens, rows), jnp.bfloat16),
            pltpu.VMEM((dp_size, tokens, columns), jnp.bfloat16),
            pltpu.VMEM((rows // 16, columns), jnp.int32),
            blocks,
            blocks,
            full,
            full,
            pltpu.VMEM((4, HALF, HALF), jnp.bfloat16),
            pltpu.VMEM((len(RELAYED), BLOCK, BLOCK), jnp.bfloat16),
            pltpu.VMEM((1, LANES), jnp.int32),
            pltpu.VMEM((mp_size, 1, LANES), jnp.int32),
            pltpu.SMEM((mp_size, 1, LANES), jnp.int32),
            pltpu.SMEM((mp_size,), jnp.int32),
            pltpu.SMEM((mp_size,), jnp.int32),
            pltpu.SMEM((block_count,), jnp.float32),
            pltpu.SemaphoreType.DMA((6,)),
            pltpu.SemaphoreType.DMA((1,)),
            pltpu.SemaphoreType.DMA((1,)),
            pltpu.SemaphoreType.DMA((mp_size,)),
            pltpu.SemaphoreType.DMA((mp_size,)),
            pltpu.SemaphoreType.DMA((2, len(RELAYED))),
            pltpu.SemaphoreType.DMA((2, len(RELAYED))),
            pltpu.SemaphoreType.DMA((2, len(RELAYED))),
            pltpu.SemaphoreType.DMA((2, len(RELAYED))),
            pltpu.SemaphoreType.DMA((2, dp_size)),
            pltpu.SemaphoreType.DMA((2, dp_size)),
            pltpu.SemaphoreType.DMA((mp_size,)),
        ],
        compiler_params=pltpu.CompilerParams(
            collective_id=0, has_side_effects=True, vmem_limit_bytes=58 * 2**20
        ),
        name="exchange",
    )(owner, left_root, right_root, hidden, out_grads, mask_words)
    return pl.pallas_call(
        place_kernel,
        out_shape=jax.ShapeDtypeStruct((rows, columns), jnp.bfloat16),
        in_specs=[in_smem, any_space],
        out_specs=any_space,
        scratch_shapes=[
            blocks,
            pltpu.SemaphoreType.DMA((block_count, BLOCK // LANES)),
            pltpu.SemaphoreType.DMA((block_count,)),
        ],
        name="place",
    )(owner, scaled)


def solution(mesh):
    in_specs = (
        P(None, "dp", None),
        P("dp", "mp"),
        P(None, "mp"),
        P("dp", "mp"),
        P(("dp", "mp"), None, None),
        P(("dp", "mp"), None, None),
    )
    return jax.shard_map(
        functools.partial(body, mesh.shape["dp"], mesh.shape["mp"]),
        mesh=mesh, in_specs=in_specs, out_specs=P("dp", "mp"), check_vma=False,
    )
```

```python
import functools

import jax
import jax.numpy as jnp
from jax import lax
from jax.experimental import pallas as pl
from jax.experimental.pallas import tpu as pltpu
from jax.sharding import PartitionSpec as P

BLOCK = 512
HALF = BLOCK // 2
LANES = 128
SIDE = 4
SLOT_ROWS = BLOCK * BLOCK // LANES + 16
MESH = pl.DeviceIdType.MESH

NEAR = [(1, 0), (0, 1), (3, 0), (0, 3)]
STRAIGHT = [(2, 0), (0, 2)]
DIAGONAL = [(1, 1), (3, 3), (1, 3), (3, 1)]
FAR = [(2, 2)]
RELAYED = [
    ((2, 1), (0, 1), (2, 0)),
    ((1, 2), (1, 0), (0, 2)),
    ((2, 3), (0, 3), (2, 0)),
    ((3, 2), (3, 0), (0, 2)),
]
ORDER = [(0, 0)] + NEAR + STRAIGHT + DIAGONAL + FAR + [legs[0] for legs in RELAYED]
DIRECT = len(ORDER) - len(RELAYED)
SLOT = {displacement: slot for slot, displacement in enumerate(ORDER)}
SLOT_CODES = [
    (sum(SLOT[away % SIDE, away // SIDE] << (4 * (away - low)) for away in range(low, low + 8)) + 2**31) % 2**32 - 2**31
    for low in (0, 8)
]

KEPT_ROWS = sum(bits << (4 * code) for code, bits in enumerate((3, 5, 9, 6, 10, 12)))


def kept_rows(words):
    count, columns = words.shape
    spread = jnp.broadcast_to(words[:, None, :], (count, 16, columns)).reshape(count * 16, columns)
    row = lax.broadcasted_iota(jnp.int32, (count * 16, columns), 0)
    code = jnp.bitwise_and(lax.shift_right_logical(spread, jnp.bitwise_and(row, 15) // 4 * 3), 7)
    bits = lax.shift_right_logical(jnp.full_like(code, KEPT_ROWS), code * 4 + jnp.bitwise_and(row, 3))
    return jnp.bitwise_and(bits, 1) == 1


def exchange_kernel(
    rows, columns, dp_size, mp_size,
    owner, left_hbm, right_hbm, hidden_hbm, grads_hbm, words_hbm,
    scaled_out,
    left, right, send_slots, relay_slots, slots, hidden, grads, words, left_full, right_full, triangles,
    tile, lists, lists_smem, ranks, block_of_slot, norms,
    load_sem, list_send, list_recv, slot_send, slot_recv, hop_send, hop_recv, last_send, last_recv, gather_send, gather_recv,
):
    capacity = left.shape[0]
    down, across = owner.shape
    block_count = down * across
    blocks, kept, halfway = left.at[pl.ds(0, block_count)], left.at[pl.ds(block_count, block_count)], right
    d, m = lax.axis_index("dp"), lax.axis_index("mp")
    x, y = lax.rem(m, SIDE), m // SIDE

    def at(displacement):
        return lax.rem(y + displacement[1], SIDE) * SIDE + lax.rem(x + displacement[0], SIDE)

    expert = m * columns // (columns * SIDE)
    own_features = pl.ds(pl.multiple_of(d * rows, rows), rows)
    own_words = pl.ds(pl.multiple_of(d * (rows // 16), rows // 16), rows // 16)
    root_loads = [
        pltpu.make_async_copy(left_hbm, left, load_sem.at[0]),
        pltpu.make_async_copy(right_hbm, right, load_sem.at[1]),
    ]
    own_loads = [
        pltpu.make_async_copy(hidden_hbm.at[expert, :, own_features], hidden.at[d], load_sem.at[2]),
        pltpu.make_async_copy(grads_hbm, grads.at[d], load_sem.at[3]),
        pltpu.make_async_copy(words_hbm.at[own_words], words, load_sem.at[4]),
    ]
    for load in root_loads + own_loads:
        load.start()

    barrier = pltpu.get_barrier_semaphore()
    for step in range(1, mp_size):
        pl.semaphore_signal(barrier, inc=1, device_id=(d, lax.rem(m + step, mp_size)), device_id_type=MESH)
    for step in range(1, dp_size):
        pl.semaphore_signal(barrier, inc=1, device_id=(lax.rem(d + step, dp_size), m), device_id_type=MESH)

    targets = [owner[j // across, j % across] for j in range(block_count)]
    lane = lax.broadcasted_iota(jnp.int32, (1, LANES), 1)
    listed = jnp.full((1, LANES), -1, jnp.int32)
    for j in range(block_count):
        listed = jnp.where(lane == j, targets[j], listed)
    tile[...] = listed
    row = lax.broadcasted_iota(jnp.int32, (HALF, HALF), 0)
    column = lax.broadcasted_iota(jnp.int32, (HALF, HALF), 1)
    for k, test in enumerate((row >= column, row < column, row > column, row == column)):
        triangles[k] = jnp.where(test, 1.0, 0.0).astype(jnp.bfloat16)
    pl.semaphore_wait(barrier, mp_size - 1 + dp_size - 1)

    for step in range(1, mp_size):
        pltpu.make_async_remote_copy(
            src_ref=tile, dst_ref=lists.at[m], send_sem=list_send.at[0], recv_sem=list_recv.at[0],
            device_id=(d, lax.rem(m + step, mp_size)), device_id_type=MESH,
        ).start()
    lists[m] = listed

    gathers = []
    for step in range(1, dp_size):
        peer = lax.rem(d + step, dp_size)
        features = pl.ds(pl.multiple_of(peer * rows, rows), rows)
        for which, (source, sink) in enumerate((
            (hidden_hbm.at[expert, :, features], hidden.at[d]),
            (grads_hbm, grads.at[d]),
        )):
            copy = pltpu.make_async_remote_copy(
                src_ref=source, dst_ref=sink, send_sem=gather_send.at[which, step], recv_sem=gather_recv.at[which, step],
                device_id=(peer, m), device_id_type=MESH,
            )
            copy.start()
            gathers.append(copy)

    others = lists.at[pl.ds(0, mp_size - 1)]
    pltpu.make_async_copy(others, others, list_recv.at[0]).wait()
    to_smem = pltpu.make_async_copy(lists, lists_smem, load_sem.at[5])
    to_smem.start()

    for slot, displacement in enumerate(ORDER):
        sender = at((SIDE - displacement[0], SIDE - displacement[1]))
        block = jnp.int32(0)
        for j in range(1, block_count):
            block = jnp.where(targets[j] == sender, jnp.int32(j), block)
        block_of_slot[slot] = block
    to_smem.wait()

    def rank_step(sender, taken):
        ranks[sender] = jnp.minimum(taken, capacity - 1)
        hit = jnp.int32(0)
        for j in range(block_count):
            hit = jnp.where(lists_smem[sender, 0, j] == m, jnp.int32(1), hit)
        return taken + hit

    lax.fori_loop(0, mp_size, rank_step, jnp.int32(0))
    for load in root_loads:
        load.wait()

    def pack(displacement):
        slot = SLOT[displacement]
        rank = ranks[at(displacement)]
        place = lax.broadcasted_iota(jnp.int32, (16, LANES), 0)
        extra = jnp.zeros((16, LANES), jnp.float32)
        for q, root in enumerate((left, right)):
            a = root[rank, 0:HALF, 0:HALF]
            b = root[rank, 0:HALF, HALF:BLOCK]
            c = root[rank, HALF:BLOCK, HALF:BLOCK]
            mixed = a * triangles[0] + c * triangles[1]
            diagonal = jnp.sum((c * triangles[3]).astype(jnp.float32), axis=0, keepdims=True)
            base = q * 4 * HALF
            for half in range(2):
                lanes = slice(half * LANES, (half + 1) * LANES)
                send_slots[slot, base + half * HALF : base + (half + 1) * HALF, :] = b[:, lanes]
                send_slots[slot, base + (2 + half) * HALF : base + (3 + half) * HALF, :] = mixed[:, lanes]
                extra = jnp.where(place == 2 * q + half, diagonal[:, lanes], extra)
        send_slots[slot, SLOT_ROWS - 16 : SLOT_ROWS, :] = extra.astype(jnp.bfloat16)

    parts = [pl.ds(BLOCK * HALF // LANES, SLOT_ROWS - BLOCK * HALF // LANES), pl.ds(0, BLOCK * HALF // LANES)]
    hops = [[], []]
    for k, (displacement, first, second) in enumerate(RELAYED):
        pack(displacement)
        for p, part in enumerate(parts):
            copy = pltpu.make_async_remote_copy(
                src_ref=send_slots.at[SLOT[displacement], part], dst_ref=relay_slots.at[k, part],
                send_sem=hop_send.at[p, k], recv_sem=hop_recv.at[p, k], device_id=(d, at(first)), device_id_type=MESH,
            )
            copy.start()
            hops[p].append(copy)
    sends = []
    for displacement in NEAR + STRAIGHT + DIAGONAL + FAR:
        pack(displacement)
        slot = SLOT[displacement]
        copy = pltpu.make_async_remote_copy(
            src_ref=send_slots.at[slot], dst_ref=slots.at[slot],
            send_sem=slot_send.at[slot], recv_sem=slot_recv.at[slot], device_id=(d, at(displacement)), device_id_type=MESH,
        )
        copy.start()
        sends.append(copy)
    pack((0, 0))
    pltpu.make_async_copy(send_slots.at[0], slots.at[0], slot_recv.at[0]).start()
    for p, part in enumerate(parts):
        for k, (displacement, first, second) in enumerate(RELAYED):
            hops[p][k].wait_recv()
            slot = SLOT[displacement]
            copy = pltpu.make_async_remote_copy(
                src_ref=relay_slots.at[k, part], dst_ref=slots.at[slot, part],
                send_sem=last_send.at[p, k], recv_sem=last_recv.at[p, k], device_id=(d, at(second)), device_id_type=MESH,
            )
            copy.start()
            sends.append(copy)

    for load in own_loads:
        load.wait()
    for copy in gathers:
        copy.wait()

    def gradient_step(j, carry):
        features = pl.ds(pl.multiple_of(j // across * BLOCK, BLOCK), BLOCK)
        places = pl.ds(pl.multiple_of(lax.rem(j, across) * BLOCK, BLOCK), BLOCK)
        gradient = lax.dot_general(
            hidden[:, :, features].reshape(-1, BLOCK), grads[:, :, places].reshape(-1, BLOCK),
            (((0,), (0,)), ((), ())), preferred_element_type=jnp.float32,
        )
        in_words = pl.ds(pl.multiple_of(j // across * (BLOCK // 16), BLOCK // 16), BLOCK // 16)
        keep = jnp.where(kept_rows(words[in_words, places]), 1.0, 0.0)
        kept[j] = keep.astype(jnp.bfloat16)
        block = (gradient * keep).astype(jnp.bfloat16)
        blocks[j] = block
        wide = block.astype(jnp.float32)
        norms[j] = jnp.sum(wide * wide)
        return carry

    lax.fori_loop(0, block_count, gradient_step, 0)

    def unpack(slot, q, full):
        base = q * 4 * HALF
        part = lambda k: slots[slot, base + k * HALF : base + (k + 1) * HALF, :]
        b = jnp.concatenate([part(0), part(1)], axis=1)
        mixed = jnp.concatenate([part(2), part(3)], axis=1)
        extra = slots[slot, SLOT_ROWS - 16 : SLOT_ROWS, :].astype(jnp.float32)
        diagonal = jnp.concatenate([extra[2 * q : 2 * q + 1, :], extra[2 * q + 1 : 2 * q + 2, :]], axis=1)
        turned = mixed.T
        full[0:HALF, 0:HALF] = mixed * triangles[0] + turned * triangles[1]
        full[0:HALF, HALF:BLOCK] = b
        full[HALF:BLOCK, 0:HALF] = b.T
        full[HALF:BLOCK, HALF:BLOCK] = (
            mixed * triangles[1] + turned * triangles[2] + triangles[3] * diagonal.astype(jnp.bfloat16)
        )

    def apply_right(slot):
        unpack(slot, 1, right_full)
        block = blocks[block_of_slot[slot]]
        return jnp.dot(block, right_full[...], preferred_element_type=jnp.float32).astype(jnp.bfloat16)

    def finish(slot, right_applied):
        j = block_of_slot[slot]
        unpack(slot, 0, left_full)
        preconditioned = jnp.dot(left_full[...], right_applied, preferred_element_type=jnp.float32)
        count = BLOCK * BLOCK
        numerator = jnp.sqrt(norms[j] / count)
        denominator = jnp.sqrt(jnp.sum(preconditioned * preconditioned) / count + 1e-06)
        scaled = (preconditioned * (numerator / denominator)).astype(jnp.bfloat16) * kept[j]
        scaled_out[slot] = scaled

    def direct_step(slot, carry):
        pltpu.make_async_copy(send_slots.at[slot], slots.at[slot], slot_recv.at[slot]).wait()
        finish(slot, apply_right(slot))
        return carry

    def right_step(k, carry):
        part = parts[0]
        pltpu.make_async_copy(send_slots.at[k, part], relay_slots.at[k, part], last_recv.at[0, k]).wait()
        halfway[k] = apply_right(k + DIRECT)
        return carry

    def left_step(k, carry):
        part = parts[1]
        pltpu.make_async_copy(send_slots.at[k, part], relay_slots.at[k, part], last_recv.at[1, k]).wait()
        finish(k + DIRECT, halfway[k])
        return carry

    lax.fori_loop(0, DIRECT, direct_step, 0)
    lax.fori_loop(0, len(RELAYED), right_step, 0)
    lax.fori_loop(0, len(RELAYED), left_step, 0)
    pltpu.make_async_copy(others, others, list_send.at[0]).wait()
    for hop in hops[0] + hops[1]:
        hop.wait_send()
    for send in sends:
        send.wait_send()


def place_kernel(owner, scaled, out, sem):
    down, across = owner.shape
    m = lax.axis_index("mp")
    copies = []
    for j in range(down * across):
        target = owner[j // across, j % across]
        away_x = lax.rem(lax.rem(m, SIDE) - lax.rem(target, SIDE) + SIDE, SIDE)
        away_y = lax.rem(m // SIDE - target // SIDE + SIDE, SIDE)
        away = away_y * SIDE + away_x
        slot = lax.rem(away, 8) * 4
        slot = jnp.bitwise_and(jnp.where(
            away < 8, lax.shift_right_logical(jnp.int32(SLOT_CODES[0]), slot), lax.shift_right_logical(jnp.int32(SLOT_CODES[1]), slot)
        ), 15)
        rows = pl.ds(j // across * BLOCK, BLOCK)
        columns = pl.ds(j % across * BLOCK, BLOCK)
        copies.append(pltpu.make_async_copy(scaled.at[slot], out.at[rows, columns], sem.at[j]))
        copies[-1].start()
    for copy in copies:
        copy.wait()


def body(dp_size, mp_size, hidden, out_grads, mask_words, owner, left_root, right_root):
    tokens, columns = out_grads.shape
    rows = hidden.shape[2] // dp_size
    block_count = owner.size
    any_space = pl.BlockSpec(memory_space=pl.ANY)
    in_hbm = pl.BlockSpec(memory_space=pltpu.HBM)
    in_smem = pl.BlockSpec(memory_space=pltpu.SMEM)
    blocks = pltpu.VMEM((block_count, BLOCK, BLOCK), jnp.bfloat16)
    slots = pltpu.VMEM((mp_size, SLOT_ROWS, LANES), jnp.bfloat16)
    full = pltpu.VMEM((BLOCK, BLOCK), jnp.bfloat16)
    scaled = pl.pallas_call(
        functools.partial(exchange_kernel, rows, columns, dp_size, mp_size),
        out_shape=pltpu.VMEM((mp_size, BLOCK, BLOCK), jnp.bfloat16),
        in_specs=[in_smem] + [in_hbm] * 5,
        out_specs=pl.BlockSpec(memory_space=pltpu.VMEM),
        scratch_shapes=[
            pltpu.VMEM(left_root.shape, jnp.bfloat16),
            pltpu.VMEM(right_root.shape, jnp.bfloat16),
            slots,
            pltpu.VMEM((len(RELAYED), SLOT_ROWS, LANES), jnp.bfloat16),
            slots,
            pltpu.VMEM((dp_size, tokens, rows), jnp.bfloat16),
            pltpu.VMEM((dp_size, tokens, columns), jnp.bfloat16),
            pltpu.VMEM((rows // 16, columns), jnp.int32),
            full,
            full,
            pltpu.VMEM((4, HALF, HALF), jnp.bfloat16),
            pltpu.VMEM((1, LANES), jnp.int32),
            pltpu.VMEM((mp_size, 1, LANES), jnp.int32),
            pltpu.SMEM((mp_size, 1, LANES), jnp.int32),
            pltpu.SMEM((mp_size,), jnp.int32),
            pltpu.SMEM((mp_size,), jnp.int32),
            pltpu.SMEM((block_count,), jnp.float32),
            pltpu.SemaphoreType.DMA((6,)),
            pltpu.SemaphoreType.DMA((1,)),
            pltpu.SemaphoreType.DMA((1,)),
            pltpu.SemaphoreType.DMA((mp_size,)),
            pltpu.SemaphoreType.DMA((mp_size,)),
            pltpu.SemaphoreType.DMA((2, len(RELAYED))),
            pltpu.SemaphoreType.DMA((2, len(RELAYED))),
            pltpu.SemaphoreType.DMA((2, len(RELAYED))),
            pltpu.SemaphoreType.DMA((2, len(RELAYED))),
            pltpu.SemaphoreType.DMA((2, dp_size)),
            pltpu.SemaphoreType.DMA((2, dp_size)),
        ],
        compiler_params=pltpu.CompilerParams(
            collective_id=0, has_side_effects=True, vmem_limit_bytes=58458112
        ),
        name="exchange",
    )(owner, left_root, right_root, hidden, out_grads, mask_words)
    return pl.pallas_call(
        place_kernel,
        out_shape=jax.ShapeDtypeStruct((rows, columns), jnp.bfloat16),
        in_specs=[in_smem, any_space],
        out_specs=any_space,
        scratch_shapes=[
            pltpu.SemaphoreType.DMA((block_count,)),
        ],
        compiler_params=pltpu.CompilerParams(vmem_limit_bytes=2**20),
        name="place",
    )(owner, scaled)


def solution(mesh):
    in_specs = (
        P(None, "dp", None),
        P("dp", "mp"),
        P(None, "mp"),
        P("dp", "mp"),
        P(("dp", "mp"), None, None),
        P(("dp", "mp"), None, None),
    )
    return jax.shard_map(
        functools.partial(body, mesh.shape["dp"], mesh.shape["mp"]),
        mesh=mesh, in_specs=in_specs, out_specs=P("dp", "mp"), check_vma=False,
    )
```

```python
import functools

import jax
import jax.numpy as jnp
from jax import lax
from jax.experimental import pallas as pl
from jax.experimental.pallas import tpu as pltpu
from jax.sharding import PartitionSpec as P

BLOCK = 512
HALF = BLOCK // 2
LANES = 128
SIDE = 4
SLOT_ROWS = BLOCK * BLOCK // LANES + 16
MESH = pl.DeviceIdType.MESH

NEAR = [(1, 0), (0, 1), (3, 0), (0, 3)]
STRAIGHT = [(2, 0), (0, 2)]
DIAGONAL = [(1, 1), (3, 3), (1, 3), (3, 1)]
FAR = [(2, 2)]
RELAYED = [
    ((2, 1), (0, 1), (2, 0)),
    ((1, 2), (1, 0), (0, 2)),
    ((2, 3), (0, 3), (2, 0)),
    ((3, 2), (3, 0), (0, 2)),
]
ORDER = [(0, 0)] + NEAR + STRAIGHT + DIAGONAL + FAR + [legs[0] for legs in RELAYED]
DIRECT = len(ORDER) - len(RELAYED)
SLOT = {displacement: slot for slot, displacement in enumerate(ORDER)}
SLOT_CODES = [
    (sum(SLOT[away % SIDE, away // SIDE] << (4 * (away - low)) for away in range(low, low + 8)) + 2**31) % 2**32 - 2**31
    for low in (0, 8)
]

KEPT_ROWS = sum(bits << (4 * code) for code, bits in enumerate((3, 5, 9, 6, 10, 12)))


def kept_rows(words):
    count, columns = words.shape
    spread = jnp.broadcast_to(words[:, None, :], (count, 16, columns)).reshape(count * 16, columns)
    row = lax.broadcasted_iota(jnp.int32, (count * 16, columns), 0)
    code = jnp.bitwise_and(lax.shift_right_logical(spread, jnp.bitwise_and(row, 15) // 4 * 3), 7)
    bits = lax.shift_right_logical(jnp.full_like(code, KEPT_ROWS), code * 4 + jnp.bitwise_and(row, 3))
    return jnp.bitwise_and(bits, 1) == 1


def exchange_kernel(
    rows, columns, dp_size, mp_size,
    owner, left_hbm, right_hbm, hidden_hbm, grads_hbm, words_hbm,
    scaled_out,
    left, right, send_slots, relay_slots, slots, hidden, grads, words, left_full, right_full, triangles,
    tile, lists, ranks, block_of_slot, norms,
    load_sem, list_send, list_recv, slot_send, slot_recv, hop_send, hop_recv, last_send, last_recv, gather_send, gather_recv,
):
    capacity = left.shape[0]
    down, across = owner.shape
    block_count = down * across
    blocks, kept, halfway = left.at[pl.ds(0, block_count)], left.at[pl.ds(block_count, block_count)], right
    d, m = lax.axis_index("dp"), lax.axis_index("mp")
    x, y = lax.rem(m, SIDE), m // SIDE

    def at(displacement):
        return lax.rem(y + displacement[1], SIDE) * SIDE + lax.rem(x + displacement[0], SIDE)

    expert = m * columns // (columns * SIDE)
    own_features = pl.ds(pl.multiple_of(d * rows, rows), rows)
    own_words = pl.ds(pl.multiple_of(d * (rows // 16), rows // 16), rows // 16)
    barrier = pltpu.get_barrier_semaphore()
    for step in range(1, mp_size):
        pl.semaphore_signal(barrier, inc=1, device_id=(d, lax.rem(m + step, mp_size)), device_id_type=MESH)
    for step in range(1, dp_size):
        pl.semaphore_signal(barrier, inc=1, device_id=(lax.rem(d + step, dp_size), m), device_id_type=MESH)

    root_loads = [
        pltpu.make_async_copy(left_hbm, left, load_sem.at[0]),
        pltpu.make_async_copy(right_hbm, right, load_sem.at[1]),
    ]
    own_loads = [
        pltpu.make_async_copy(hidden_hbm.at[expert, :, own_features], hidden.at[d], load_sem.at[2]),
        pltpu.make_async_copy(grads_hbm, grads.at[d], load_sem.at[3]),
        pltpu.make_async_copy(words_hbm.at[own_words], words, load_sem.at[4]),
    ]
    for load in root_loads + own_loads:
        load.start()

    targets = [owner[j // across, j % across] for j in range(block_count)]
    for j in range(block_count):
        tile[0, j] = targets[j]

    def clear(j, carry):
        tile[0, j] = jnp.int32(-1)
        return carry

    lax.fori_loop(block_count, LANES, clear, 0)
    row = lax.broadcasted_iota(jnp.int32, (HALF, HALF), 0)
    column = lax.broadcasted_iota(jnp.int32, (HALF, HALF), 1)
    for k, test in enumerate((row >= column, row < column, row > column, row == column)):
        triangles[k] = jnp.where(test, 1.0, 0.0).astype(jnp.bfloat16)
    pl.semaphore_wait(barrier, mp_size - 1 + dp_size - 1)

    for displacement in FAR + [legs[0] for legs in RELAYED] + DIAGONAL + STRAIGHT + NEAR:
        pltpu.make_async_remote_copy(
            src_ref=tile, dst_ref=lists.at[m], send_sem=list_send.at[0], recv_sem=list_recv.at[0],
            device_id=(d, at(displacement)), device_id_type=MESH,
        ).start()
    for j in range(block_count):
        lists[m, 0, j] = targets[j]

    gathers = []
    for step in range(1, dp_size):
        peer = lax.rem(d + step, dp_size)
        features = pl.ds(pl.multiple_of(peer * rows, rows), rows)
        for which, (source, sink) in enumerate((
            (hidden_hbm.at[expert, :, features], hidden.at[d]),
            (grads_hbm, grads.at[d]),
        )):
            copy = pltpu.make_async_remote_copy(
                src_ref=source, dst_ref=sink, send_sem=gather_send.at[which, step], recv_sem=gather_recv.at[which, step],
                device_id=(peer, m), device_id_type=MESH,
            )
            copy.start()
            gathers.append(copy)

    others = lists.at[pl.ds(0, mp_size - 1)]
    pltpu.make_async_copy(others, others, list_recv.at[0]).wait()
    for slot, displacement in enumerate(ORDER):
        sender = at((SIDE - displacement[0], SIDE - displacement[1]))
        block = jnp.int32(0)
        for j in range(1, block_count):
            block = jnp.where(targets[j] == sender, jnp.int32(j), block)
        block_of_slot[slot] = block

    def rank_step(sender, taken):
        ranks[sender] = jnp.minimum(taken, capacity - 1)
        hit = jnp.int32(0)
        for j in range(block_count):
            hit = jnp.where(lists[sender, 0, j] == m, jnp.int32(1), hit)
        return taken + hit

    lax.fori_loop(0, mp_size, rank_step, jnp.int32(0))
    for load in root_loads:
        load.wait()

    def pack(displacement, halves=(1, 0)):
        slot = SLOT[displacement]
        rank = ranks[at(displacement)]
        for q in halves:
            root = (left, right)[q]
            b = root[rank, 0:HALF, HALF:BLOCK]
            mixed = root[rank, 0:HALF, 0:HALF] * triangles[0] + root[rank, HALF:BLOCK, HALF:BLOCK] * triangles[1]
            base = q * 4 * HALF
            for half in range(2):
                lanes = slice(half * LANES, (half + 1) * LANES)
                send_slots[slot, base + half * HALF : base + (half + 1) * HALF, :] = b[:, lanes]
                send_slots[slot, base + (2 + half) * HALF : base + (3 + half) * HALF, :] = mixed[:, lanes]
        if 1 in halves:
            place = lax.broadcasted_iota(jnp.int32, (16, LANES), 0)
            extra = jnp.zeros((16, LANES), jnp.float32)
            for q, root in enumerate((left, right)):
                last = (root[rank, HALF:BLOCK, HALF:BLOCK] * triangles[3]).astype(jnp.float32)
                diagonal = jnp.sum(last, axis=0, keepdims=True)
                for half in range(2):
                    extra = jnp.where(place == 2 * q + half, diagonal[:, half * LANES : (half + 1) * LANES], extra)
            send_slots[slot, SLOT_ROWS - 16 : SLOT_ROWS, :] = extra.astype(jnp.bfloat16)

    parts = [pl.ds(BLOCK * HALF // LANES, SLOT_ROWS - BLOCK * HALF // LANES), pl.ds(0, BLOCK * HALF // LANES)]
    hops = [[], []]
    for p, part in enumerate(parts):
        for k, (displacement, first, second) in enumerate(RELAYED):
            pack(displacement, (1 - p,))
            copy = pltpu.make_async_remote_copy(
                src_ref=send_slots.at[SLOT[displacement], part], dst_ref=relay_slots.at[k, part],
                send_sem=hop_send.at[p, k], recv_sem=hop_recv.at[p, k], device_id=(d, at(first)), device_id_type=MESH,
            )
            copy.start()
            hops[p].append(copy)
    sends = []
    for displacement in NEAR + STRAIGHT + DIAGONAL + FAR:
        pack(displacement)
        slot = SLOT[displacement]
        copy = pltpu.make_async_remote_copy(
            src_ref=send_slots.at[slot], dst_ref=slots.at[slot],
            send_sem=slot_send.at[slot], recv_sem=slot_recv.at[slot], device_id=(d, at(displacement)), device_id_type=MESH,
        )
        copy.start()
        sends.append(copy)
    pack((0, 0))
    pltpu.make_async_copy(send_slots.at[0], slots.at[0], slot_recv.at[0]).start()
    for p, part in enumerate(parts):
        for k, (displacement, first, second) in enumerate(RELAYED):
            hops[p][k].wait_recv()
            slot = SLOT[displacement]
            copy = pltpu.make_async_remote_copy(
                src_ref=relay_slots.at[k, part], dst_ref=slots.at[slot, part],
                send_sem=last_send.at[p, k], recv_sem=last_recv.at[p, k], device_id=(d, at(second)), device_id_type=MESH,
            )
            copy.start()
            sends.append(copy)

    for load in own_loads:
        load.wait()
    for copy in gathers:
        copy.wait()

    def gradient_step(j, carry):
        features = pl.ds(pl.multiple_of(j // across * BLOCK, BLOCK), BLOCK)
        places = pl.ds(pl.multiple_of(lax.rem(j, across) * BLOCK, BLOCK), BLOCK)
        gradient = lax.dot_general(
            hidden[:, :, features].reshape(-1, BLOCK), grads[:, :, places].reshape(-1, BLOCK),
            (((0,), (0,)), ((), ())), preferred_element_type=jnp.float32,
        )
        in_words = pl.ds(pl.multiple_of(j // across * (BLOCK // 16), BLOCK // 16), BLOCK // 16)
        keep = jnp.where(kept_rows(words[in_words, places]), 1.0, 0.0)
        kept[j] = keep.astype(jnp.bfloat16)
        block = (gradient * keep).astype(jnp.bfloat16)
        blocks[j] = block
        wide = block.astype(jnp.float32)
        norms[j] = jnp.sum(wide * wide)
        return carry

    lax.fori_loop(0, block_count, gradient_step, 0)

    def unpack(slot, q, full):
        base = q * 4 * HALF
        part = lambda k: slots[slot, base + k * HALF : base + (k + 1) * HALF, :]
        b = jnp.concatenate([part(0), part(1)], axis=1)
        mixed = jnp.concatenate([part(2), part(3)], axis=1)
        extra = slots[slot, SLOT_ROWS - 16 : SLOT_ROWS, :].astype(jnp.float32)
        diagonal = jnp.concatenate([extra[2 * q : 2 * q + 1, :], extra[2 * q + 1 : 2 * q + 2, :]], axis=1)
        turned = mixed.T
        full[0:HALF, 0:HALF] = mixed * triangles[0] + turned * triangles[1]
        full[0:HALF, HALF:BLOCK] = b
        full[HALF:BLOCK, 0:HALF] = b.T
        full[HALF:BLOCK, HALF:BLOCK] = (
            mixed * triangles[1] + turned * triangles[2] + triangles[3] * diagonal.astype(jnp.bfloat16)
        )

    def apply_right(slot):
        unpack(slot, 1, right_full)
        block = blocks[block_of_slot[slot]]
        return jnp.dot(block, right_full[...], preferred_element_type=jnp.float32).astype(jnp.bfloat16)

    def finish(slot, right_applied):
        j = block_of_slot[slot]
        unpack(slot, 0, left_full)
        preconditioned = jnp.dot(left_full[...], right_applied, preferred_element_type=jnp.float32)
        count = BLOCK * BLOCK
        numerator = jnp.sqrt(norms[j] / count)
        denominator = jnp.sqrt(jnp.sum(preconditioned * preconditioned) / count + 1e-06)
        scaled = (preconditioned * (numerator / denominator)).astype(jnp.bfloat16) * kept[j]
        scaled_out[slot] = scaled

    def direct_step(slot, carry):
        pltpu.make_async_copy(send_slots.at[slot], slots.at[slot], slot_recv.at[slot]).wait()
        finish(slot, apply_right(slot))
        return carry

    def right_step(k, carry):
        part = parts[0]
        pltpu.make_async_copy(send_slots.at[k, part], relay_slots.at[k, part], last_recv.at[0, k]).wait()
        halfway[k] = apply_right(k + DIRECT)
        return carry

    def left_step(k, carry):
        part = parts[1]
        pltpu.make_async_copy(send_slots.at[k, part], relay_slots.at[k, part], last_recv.at[1, k]).wait()
        finish(k + DIRECT, halfway[k])
        return carry

    lax.fori_loop(0, DIRECT, direct_step, 0)
    lax.fori_loop(0, len(RELAYED), right_step, 0)
    lax.fori_loop(0, len(RELAYED), left_step, 0)
    pltpu.make_async_copy(others, others, list_send.at[0]).wait()
    for hop in hops[0] + hops[1]:
        hop.wait_send()
    for send in sends:
        send.wait_send()


def place_kernel(owner, scaled, out, sem):
    down, across = owner.shape
    m = lax.axis_index("mp")
    copies = []
    for j in range(down * across):
        target = owner[j // across, j % across]
        away_x = lax.rem(lax.rem(m, SIDE) - lax.rem(target, SIDE) + SIDE, SIDE)
        away_y = lax.rem(m // SIDE - target // SIDE + SIDE, SIDE)
        away = away_y * SIDE + away_x
        slot = lax.rem(away, 8) * 4
        slot = jnp.bitwise_and(jnp.where(
            away < 8, lax.shift_right_logical(jnp.int32(SLOT_CODES[0]), slot), lax.shift_right_logical(jnp.int32(SLOT_CODES[1]), slot)
        ), 15)
        rows = pl.ds(j // across * BLOCK, BLOCK)
        columns = pl.ds(j % across * BLOCK, BLOCK)
        copies.append(pltpu.make_async_copy(scaled.at[slot], out.at[rows, columns], sem.at[j]))
        copies[-1].start()
    for copy in copies:
        copy.wait()


def body(dp_size, mp_size, hidden, out_grads, mask_words, owner, left_root, right_root):
    tokens, columns = out_grads.shape
    rows = hidden.shape[2] // dp_size
    block_count = owner.size
    any_space = pl.BlockSpec(memory_space=pl.ANY)
    in_hbm = pl.BlockSpec(memory_space=pltpu.HBM)
    in_smem = pl.BlockSpec(memory_space=pltpu.SMEM)
    blocks = pltpu.VMEM((block_count, BLOCK, BLOCK), jnp.bfloat16)
    slots = pltpu.VMEM((mp_size, SLOT_ROWS, LANES), jnp.bfloat16)
    full = pltpu.VMEM((BLOCK, BLOCK), jnp.bfloat16)
    scaled = pl.pallas_call(
        functools.partial(exchange_kernel, rows, columns, dp_size, mp_size),
        out_shape=pltpu.VMEM((mp_size, BLOCK, BLOCK), jnp.bfloat16),
        in_specs=[in_smem] + [in_hbm] * 5,
        out_specs=pl.BlockSpec(memory_space=pltpu.VMEM),
        scratch_shapes=[
            pltpu.VMEM(left_root.shape, jnp.bfloat16),
            pltpu.VMEM(right_root.shape, jnp.bfloat16),
            slots,
            pltpu.VMEM((len(RELAYED), SLOT_ROWS, LANES), jnp.bfloat16),
            slots,
            pltpu.VMEM((dp_size, tokens, rows), jnp.bfloat16),
            pltpu.VMEM((dp_size, tokens, columns), jnp.bfloat16),
            pltpu.VMEM((rows // 16, columns), jnp.int32),
            full,
            full,
            pltpu.VMEM((4, HALF, HALF), jnp.bfloat16),
            pltpu.SMEM((1, LANES), jnp.int32),
            pltpu.SMEM((mp_size, 1, LANES), jnp.int32),
            pltpu.SMEM((mp_size,), jnp.int32),
            pltpu.SMEM((mp_size,), jnp.int32),
            pltpu.SMEM((block_count,), jnp.float32),
            pltpu.SemaphoreType.DMA((6,)),
            pltpu.SemaphoreType.DMA((1,)),
            pltpu.SemaphoreType.DMA((1,)),
            pltpu.SemaphoreType.DMA((mp_size,)),
            pltpu.SemaphoreType.DMA((mp_size,)),
            pltpu.SemaphoreType.DMA((2, len(RELAYED))),
            pltpu.SemaphoreType.DMA((2, len(RELAYED))),
            pltpu.SemaphoreType.DMA((2, len(RELAYED))),
            pltpu.SemaphoreType.DMA((2, len(RELAYED))),
            pltpu.SemaphoreType.DMA((2, dp_size)),
            pltpu.SemaphoreType.DMA((2, dp_size)),
        ],
        compiler_params=pltpu.CompilerParams(
            collective_id=0, has_side_effects=True, vmem_limit_bytes=58458112
        ),
        name="exchange",
    )(owner, left_root, right_root, hidden, out_grads, mask_words)
    return pl.pallas_call(
        place_kernel,
        out_shape=jax.ShapeDtypeStruct((rows, columns), jnp.bfloat16),
        in_specs=[in_smem, any_space],
        out_specs=any_space,
        scratch_shapes=[
            pltpu.SemaphoreType.DMA((block_count,)),
        ],
        compiler_params=pltpu.CompilerParams(vmem_limit_bytes=2**20),
        name="place",
    )(owner, scaled)


def solution(mesh):
    in_specs = (
        P(None, "dp", None),
        P("dp", "mp"),
        P(None, "mp"),
        P("dp", "mp"),
        P(("dp", "mp"), None, None),
        P(("dp", "mp"), None, None),
    )
    return jax.shard_map(
        functools.partial(body, mesh.shape["dp"], mesh.shape["mp"]),
        mesh=mesh, in_specs=in_specs, out_specs=P("dp", "mp"), check_vma=False,
    )
```

```python
import functools

import jax
import jax.numpy as jnp
from jax import lax
from jax.experimental import pallas as pl
from jax.experimental.pallas import tpu as pltpu
from jax.sharding import PartitionSpec as P

BLOCK = 512
HALF = BLOCK // 2
LANES = 128
SIDE = 4
SLOT_ROWS = BLOCK * BLOCK // LANES + 16
MESH = pl.DeviceIdType.MESH

NEAR = [(1, 0), (0, 1), (3, 0), (0, 3)]
STRAIGHT = [(2, 0), (0, 2)]
DIAGONAL = [(1, 1), (3, 3), (1, 3), (3, 1)]
FAR = [(2, 2)]
RELAYED = [
    ((2, 1), (0, 1), (2, 0)),
    ((1, 2), (1, 0), (0, 2)),
    ((2, 3), (0, 3), (2, 0)),
    ((3, 2), (3, 0), (0, 2)),
]
ORDER = [(0, 0)] + NEAR + DIAGONAL + FAR + STRAIGHT + [legs[0] for legs in RELAYED]
DIRECT = len(ORDER) - len(RELAYED)
SLOT = {displacement: slot for slot, displacement in enumerate(ORDER)}
SLOT_CODES = [
    (sum(SLOT[away % SIDE, away // SIDE] << (4 * (away - low)) for away in range(low, low + 8)) + 2**31) % 2**32 - 2**31
    for low in (0, 8)
]

KEPT_ROWS = sum(bits << (4 * code) for code, bits in enumerate((3, 5, 9, 6, 10, 12)))


def kept_rows(words):
    count, columns = words.shape
    spread = jnp.broadcast_to(words[:, None, :], (count, 16, columns)).reshape(count * 16, columns)
    row = lax.broadcasted_iota(jnp.int32, (count * 16, columns), 0)
    code = jnp.bitwise_and(lax.shift_right_logical(spread, jnp.bitwise_and(row, 15) // 4 * 3), 7)
    bits = lax.shift_right_logical(jnp.full_like(code, KEPT_ROWS), code * 4 + jnp.bitwise_and(row, 3))
    return jnp.bitwise_and(bits, 1) == 1


def exchange_kernel(
    rows, columns, dp_size, mp_size,
    owner, left_hbm, right_hbm, hidden_hbm, grads_hbm, words_hbm,
    scaled_out,
    left, right, send_slots, relay_slots, slots, hidden, grads, words, left_full, right_full, triangles,
    tile, lists, ranks, block_of_slot, norms,
    load_sem, list_send, list_recv, slot_send, slot_recv, hop_send, hop_recv, last_send, last_recv, gather_send, gather_recv,
):
    capacity = left.shape[0]
    down, across = owner.shape
    block_count = down * across
    blocks, kept, halfway = left.at[pl.ds(0, block_count)], left.at[pl.ds(block_count, block_count)], right
    d, m = lax.axis_index("dp"), lax.axis_index("mp")
    x, y = lax.rem(m, SIDE), m // SIDE

    def at(displacement):
        return lax.rem(y + displacement[1], SIDE) * SIDE + lax.rem(x + displacement[0], SIDE)

    expert = m * columns // (columns * SIDE)
    own_features = pl.ds(pl.multiple_of(d * rows, rows), rows)
    own_words = pl.ds(pl.multiple_of(d * (rows // 16), rows // 16), rows // 16)
    barrier = pltpu.get_barrier_semaphore()
    for step in range(1, mp_size):
        pl.semaphore_signal(barrier, inc=1, device_id=(d, lax.rem(m + step, mp_size)), device_id_type=MESH)
    for step in range(1, dp_size):
        pl.semaphore_signal(barrier, inc=1, device_id=(lax.rem(d + step, dp_size), m), device_id_type=MESH)

    root_loads = [
        pltpu.make_async_copy(left_hbm, left, load_sem.at[0]),
        pltpu.make_async_copy(right_hbm, right, load_sem.at[1]),
    ]
    own_loads = [
        pltpu.make_async_copy(hidden_hbm.at[expert, :, own_features], hidden.at[d], load_sem.at[2]),
        pltpu.make_async_copy(grads_hbm, grads.at[d], load_sem.at[3]),
        pltpu.make_async_copy(words_hbm.at[own_words], words, load_sem.at[4]),
    ]
    for load in root_loads + own_loads:
        load.start()

    targets = [owner[j // across, j % across] for j in range(block_count)]
    for j in range(block_count):
        tile[0, j] = targets[j]

    def clear(j, carry):
        tile[0, j] = jnp.int32(-1)
        return carry

    lax.fori_loop(block_count, LANES, clear, 0)
    row = lax.broadcasted_iota(jnp.int32, (HALF, HALF), 0)
    column = lax.broadcasted_iota(jnp.int32, (HALF, HALF), 1)
    for k, test in enumerate((row >= column, row < column, row > column, row == column)):
        triangles[k] = jnp.where(test, 1.0, 0.0).astype(jnp.bfloat16)
    pl.semaphore_wait(barrier, mp_size - 1 + dp_size - 1)

    for displacement in FAR + [legs[0] for legs in RELAYED] + DIAGONAL + STRAIGHT + NEAR:
        pltpu.make_async_remote_copy(
            src_ref=tile, dst_ref=lists.at[m], send_sem=list_send.at[0], recv_sem=list_recv.at[0],
            device_id=(d, at(displacement)), device_id_type=MESH,
        ).start()
    for j in range(block_count):
        lists[m, 0, j] = targets[j]

    gathers = []
    for step in range(1, dp_size):
        peer = lax.rem(d + step, dp_size)
        features = pl.ds(pl.multiple_of(peer * rows, rows), rows)
        for which, (source, sink) in enumerate((
            (hidden_hbm.at[expert, :, features], hidden.at[d]),
            (grads_hbm, grads.at[d]),
        )):
            copy = pltpu.make_async_remote_copy(
                src_ref=source, dst_ref=sink, send_sem=gather_send.at[which, step], recv_sem=gather_recv.at[which, step],
                device_id=(peer, m), device_id_type=MESH,
            )
            copy.start()
            gathers.append(copy)

    others = lists.at[pl.ds(0, mp_size - 1)]
    pltpu.make_async_copy(others, others, list_recv.at[0]).wait()
    for slot, displacement in enumerate(ORDER):
        sender = at((SIDE - displacement[0], SIDE - displacement[1]))
        block = jnp.int32(0)
        for j in range(1, block_count):
            block = jnp.where(targets[j] == sender, jnp.int32(j), block)
        block_of_slot[slot] = block

    def rank_step(sender, taken):
        ranks[sender] = jnp.minimum(taken, capacity - 1)
        hit = jnp.int32(0)
        for j in range(block_count):
            hit = jnp.where(lists[sender, 0, j] == m, jnp.int32(1), hit)
        return taken + hit

    lax.fori_loop(0, mp_size, rank_step, jnp.int32(0))
    for load in root_loads:
        load.wait()

    def pack(displacement, halves=(1, 0)):
        slot = SLOT[displacement]
        rank = ranks[at(displacement)]
        for q in halves:
            root = (left, right)[q]
            b = root[rank, 0:HALF, HALF:BLOCK]
            mixed = root[rank, 0:HALF, 0:HALF] * triangles[0] + root[rank, HALF:BLOCK, HALF:BLOCK] * triangles[1]
            base = q * 4 * HALF
            for half in range(2):
                lanes = slice(half * LANES, (half + 1) * LANES)
                send_slots[slot, base + half * HALF : base + (half + 1) * HALF, :] = b[:, lanes]
                send_slots[slot, base + (2 + half) * HALF : base + (3 + half) * HALF, :] = mixed[:, lanes]
        if 1 in halves:
            place = lax.broadcasted_iota(jnp.int32, (16, LANES), 0)
            extra = jnp.zeros((16, LANES), jnp.float32)
            for q, root in enumerate((left, right)):
                last = (root[rank, HALF:BLOCK, HALF:BLOCK] * triangles[3]).astype(jnp.float32)
                diagonal = jnp.sum(last, axis=0, keepdims=True)
                for half in range(2):
                    extra = jnp.where(place == 2 * q + half, diagonal[:, half * LANES : (half + 1) * LANES], extra)
            send_slots[slot, SLOT_ROWS - 16 : SLOT_ROWS, :] = extra.astype(jnp.bfloat16)

    parts = [pl.ds(BLOCK * HALF // LANES, SLOT_ROWS - BLOCK * HALF // LANES), pl.ds(0, BLOCK * HALF // LANES)]
    hops = [[], []]
    for p, part in enumerate(parts):
        for k, (displacement, first, second) in enumerate(RELAYED):
            pack(displacement, (1 - p,))
            copy = pltpu.make_async_remote_copy(
                src_ref=send_slots.at[SLOT[displacement], part], dst_ref=relay_slots.at[k, part],
                send_sem=hop_send.at[p, k], recv_sem=hop_recv.at[p, k], device_id=(d, at(first)), device_id_type=MESH,
            )
            copy.start()
            hops[p].append(copy)
    sends = []
    for displacement in NEAR + DIAGONAL + FAR + STRAIGHT:
        pack(displacement)
        slot = SLOT[displacement]
        copy = pltpu.make_async_remote_copy(
            src_ref=send_slots.at[slot], dst_ref=slots.at[slot],
            send_sem=slot_send.at[slot], recv_sem=slot_recv.at[slot], device_id=(d, at(displacement)), device_id_type=MESH,
        )
        copy.start()
        sends.append(copy)
    pack((0, 0))
    pltpu.make_async_copy(send_slots.at[0], slots.at[0], slot_recv.at[0]).start()
    forwards = []
    for p, part in enumerate(parts):
        for k, (displacement, first, second) in enumerate(RELAYED):
            hops[p][k].wait_recv()
            slot = SLOT[displacement]
            copy = pltpu.make_async_remote_copy(
                src_ref=relay_slots.at[k, part], dst_ref=slots.at[slot, part],
                send_sem=last_send.at[p, k], recv_sem=last_recv.at[p, k], device_id=(d, at(second)), device_id_type=MESH,
            )
            copy.start()
            forwards.append(copy)

    for load in own_loads:
        load.wait()
    for copy in gathers:
        copy.wait()

    def gradient_step(j, carry):
        features = pl.ds(pl.multiple_of(j // across * BLOCK, BLOCK), BLOCK)
        places = pl.ds(pl.multiple_of(lax.rem(j, across) * BLOCK, BLOCK), BLOCK)
        gradient = lax.dot_general(
            hidden[:, :, features].reshape(-1, BLOCK), grads[:, :, places].reshape(-1, BLOCK),
            (((0,), (0,)), ((), ())), preferred_element_type=jnp.float32,
        )
        in_words = pl.ds(pl.multiple_of(j // across * (BLOCK // 16), BLOCK // 16), BLOCK // 16)
        keep = jnp.where(kept_rows(words[in_words, places]), 1.0, 0.0)
        kept[j] = keep.astype(jnp.bfloat16)
        block = (gradient * keep).astype(jnp.bfloat16)
        blocks[j] = block
        wide = block.astype(jnp.float32)
        norms[j] = jnp.sum(wide * wide)
        return carry

    lax.fori_loop(0, block_count, gradient_step, 0)

    def unpack(slot, q, full):
        base = q * 4 * HALF
        part = lambda k: slots[slot, base + k * HALF : base + (k + 1) * HALF, :]
        b = jnp.concatenate([part(0), part(1)], axis=1)
        mixed = jnp.concatenate([part(2), part(3)], axis=1)
        extra = slots[slot, SLOT_ROWS - 16 : SLOT_ROWS, :].astype(jnp.float32)
        diagonal = jnp.concatenate([extra[2 * q : 2 * q + 1, :], extra[2 * q + 1 : 2 * q + 2, :]], axis=1)
        turned = mixed.T
        full[0:HALF, 0:HALF] = mixed * triangles[0] + turned * triangles[1]
        full[0:HALF, HALF:BLOCK] = b
        full[HALF:BLOCK, 0:HALF] = b.T
        full[HALF:BLOCK, HALF:BLOCK] = (
            mixed * triangles[1] + turned * triangles[2] + triangles[3] * diagonal.astype(jnp.bfloat16)
        )

    def apply_right(slot):
        unpack(slot, 1, right_full)
        block = blocks[block_of_slot[slot]]
        return jnp.dot(block, right_full[...], preferred_element_type=jnp.float32).astype(jnp.bfloat16)

    def scale(slot, preconditioned):
        j = block_of_slot[slot]
        count = BLOCK * BLOCK
        numerator = jnp.sqrt(norms[j] / count)
        denominator = jnp.sqrt(jnp.sum(preconditioned * preconditioned) / count + 1e-06)
        scaled_out[slot] = (preconditioned * (numerator / denominator)).astype(jnp.bfloat16) * kept[j]

    def finish(slot, right_applied):
        unpack(slot, 0, left_full)
        scale(slot, jnp.dot(left_full[...], right_applied, preferred_element_type=jnp.float32))

    def direct_step(slot, carry):
        pltpu.make_async_copy(send_slots.at[slot], slots.at[slot], slot_recv.at[slot]).wait()
        finish(slot, apply_right(slot))
        return carry

    def right_step(k, carry):
        part = parts[0]
        pltpu.make_async_copy(send_slots.at[k, part], relay_slots.at[k, part], last_recv.at[0, k]).wait()
        halfway[k] = apply_right(k + DIRECT)
        return carry

    def left_step(pair, carry):
        part = parts[1]
        both = ((2 * pair, left_full), (2 * pair + 1, right_full))
        for k, full in both:
            pltpu.make_async_copy(send_slots.at[k, part], relay_slots.at[k, part], last_recv.at[1, k]).wait()
            unpack(k + DIRECT, 0, full)
        products = [jnp.dot(full[...], halfway[k], preferred_element_type=jnp.float32) for k, full in both]
        for (k, _), product in zip(both, products):
            scale(k + DIRECT, product)
        return carry

    lax.fori_loop(0, DIRECT, direct_step, 0)
    lax.fori_loop(0, len(RELAYED), right_step, 0)
    pltpu.make_async_copy(others, others, list_send.at[0]).wait()
    for copy in hops[0] + hops[1] + sends:
        copy.wait_send()
    lax.fori_loop(0, len(RELAYED) // 2, left_step, 0)
    for copy in forwards:
        copy.wait_send()


def place_kernel(owner, scaled, out, sem):
    down, across = owner.shape
    m = lax.axis_index("mp")
    copies = []
    for j in range(down * across):
        target = owner[j // across, j % across]
        away_x = lax.rem(lax.rem(m, SIDE) - lax.rem(target, SIDE) + SIDE, SIDE)
        away_y = lax.rem(m // SIDE - target // SIDE + SIDE, SIDE)
        away = away_y * SIDE + away_x
        slot = lax.rem(away, 8) * 4
        slot = jnp.bitwise_and(jnp.where(
            away < 8, lax.shift_right_logical(jnp.int32(SLOT_CODES[0]), slot), lax.shift_right_logical(jnp.int32(SLOT_CODES[1]), slot)
        ), 15)
        rows = pl.ds(j // across * BLOCK, BLOCK)
        columns = pl.ds(j % across * BLOCK, BLOCK)
        copies.append(pltpu.make_async_copy(scaled.at[slot], out.at[rows, columns], sem.at[j]))
        copies[-1].start()
    for copy in copies:
        copy.wait()


def body(dp_size, mp_size, hidden, out_grads, mask_words, owner, left_root, right_root):
    tokens, columns = out_grads.shape
    rows = hidden.shape[2] // dp_size
    block_count = owner.size
    any_space = pl.BlockSpec(memory_space=pl.ANY)
    in_hbm = pl.BlockSpec(memory_space=pltpu.HBM)
    in_smem = pl.BlockSpec(memory_space=pltpu.SMEM)
    blocks = pltpu.VMEM((block_count, BLOCK, BLOCK), jnp.bfloat16)
    slots = pltpu.VMEM((mp_size, SLOT_ROWS, LANES), jnp.bfloat16)
    full = pltpu.VMEM((BLOCK, BLOCK), jnp.bfloat16)
    scaled = pl.pallas_call(
        functools.partial(exchange_kernel, rows, columns, dp_size, mp_size),
        out_shape=pltpu.VMEM((mp_size, BLOCK, BLOCK), jnp.bfloat16),
        in_specs=[in_smem] + [in_hbm] * 5,
        out_specs=pl.BlockSpec(memory_space=pltpu.VMEM),
        scratch_shapes=[
            pltpu.VMEM(left_root.shape, jnp.bfloat16),
            pltpu.VMEM(right_root.shape, jnp.bfloat16),
            slots,
            pltpu.VMEM((len(RELAYED), SLOT_ROWS, LANES), jnp.bfloat16),
            slots,
            pltpu.VMEM((dp_size, tokens, rows), jnp.bfloat16),
            pltpu.VMEM((dp_size, tokens, columns), jnp.bfloat16),
            pltpu.VMEM((rows // 16, columns), jnp.int32),
            full,
            full,
            pltpu.VMEM((4, HALF, HALF), jnp.bfloat16),
            pltpu.SMEM((1, LANES), jnp.int32),
            pltpu.SMEM((mp_size, 1, LANES), jnp.int32),
            pltpu.SMEM((mp_size,), jnp.int32),
            pltpu.SMEM((mp_size,), jnp.int32),
            pltpu.SMEM((block_count,), jnp.float32),
            pltpu.SemaphoreType.DMA((6,)),
            pltpu.SemaphoreType.DMA((1,)),
            pltpu.SemaphoreType.DMA((1,)),
            pltpu.SemaphoreType.DMA((mp_size,)),
            pltpu.SemaphoreType.DMA((mp_size,)),
            pltpu.SemaphoreType.DMA((2, len(RELAYED))),
            pltpu.SemaphoreType.DMA((2, len(RELAYED))),
            pltpu.SemaphoreType.DMA((2, len(RELAYED))),
            pltpu.SemaphoreType.DMA((2, len(RELAYED))),
            pltpu.SemaphoreType.DMA((2, dp_size)),
            pltpu.SemaphoreType.DMA((2, dp_size)),
        ],
        compiler_params=pltpu.CompilerParams(
            collective_id=0, has_side_effects=True, vmem_limit_bytes=58458112
        ),
        name="exchange",
    )(owner, left_root, right_root, hidden, out_grads, mask_words)
    return pl.pallas_call(
        place_kernel,
        out_shape=jax.ShapeDtypeStruct((rows, columns), jnp.bfloat16),
        in_specs=[in_smem, any_space],
        out_specs=any_space,
        scratch_shapes=[
            pltpu.SemaphoreType.DMA((block_count,)),
        ],
        compiler_params=pltpu.CompilerParams(vmem_limit_bytes=2**20),
        name="place",
    )(owner, scaled)


def solution(mesh):
    in_specs = (
        P(None, "dp", None),
        P("dp", "mp"),
        P(None, "mp"),
        P("dp", "mp"),
        P(("dp", "mp"), None, None),
        P(("dp", "mp"), None, None),
    )
    return jax.shard_map(
        functools.partial(body, mesh.shape["dp"], mesh.shape["mp"]),
        mesh=mesh, in_specs=in_specs, out_specs=P("dp", "mp"), check_vma=False,
    )
```

```python
import functools

import jax
import jax.numpy as jnp
from jax import lax
from jax.experimental import pallas as pl
from jax.experimental.pallas import tpu as pltpu
from jax.sharding import PartitionSpec as P

BLOCK = 512
HALF = BLOCK // 2
LANES = 128
SIDE = 4
SLOT_ROWS = BLOCK * BLOCK // LANES + 16
MESH = pl.DeviceIdType.MESH

NEAR = [(1, 0), (0, 1), (3, 0), (0, 3)]
STRAIGHT = [(2, 0), (0, 2)]
DIAGONAL = [(1, 1), (3, 3), (1, 3), (3, 1)]
FAR = [(2, 2)]
RELAYED = [
    ((2, 1), (0, 1), (2, 0)),
    ((1, 2), (1, 0), (0, 2)),
    ((2, 3), (0, 3), (2, 0)),
    ((3, 2), (3, 0), (0, 2)),
]
ORDER = [(0, 0)] + NEAR + DIAGONAL + FAR + STRAIGHT + [legs[0] for legs in RELAYED]
DIRECT = len(ORDER) - len(RELAYED)
SLOT = {displacement: slot for slot, displacement in enumerate(ORDER)}
SLOT_CODES = [
    (sum(SLOT[away % SIDE, away // SIDE] << (4 * (away - low)) for away in range(low, low + 8)) + 2**31) % 2**32 - 2**31
    for low in (0, 8)
]

KEPT_ROWS = sum(bits << (4 * code) for code, bits in enumerate((3, 5, 9, 6, 10, 12)))


def kept_rows(words):
    count, columns = words.shape
    spread = jnp.broadcast_to(words[:, None, :], (count, 16, columns)).reshape(count * 16, columns)
    row = lax.broadcasted_iota(jnp.int32, (count * 16, columns), 0)
    code = jnp.bitwise_and(lax.shift_right_logical(spread, jnp.bitwise_and(row, 15) // 4 * 3), 7)
    bits = lax.shift_right_logical(jnp.full_like(code, KEPT_ROWS), code * 4 + jnp.bitwise_and(row, 3))
    return jnp.bitwise_and(bits, 1) == 1


def exchange_kernel(
    rows, columns, dp_size, mp_size,
    owner, left_hbm, right_hbm, hidden_hbm, grads_hbm, words_hbm,
    scaled_out,
    left, right, send_slots, relay_slots, slots, hidden, grads, words, left_full, right_full, triangles,
    tile, lists, ranks, block_of_slot, norms,
    load_sem, list_send, list_recv, slot_send, slot_recv, hop_send, hop_recv, last_send, last_recv, gather_send, gather_recv,
):
    capacity = left.shape[0]
    down, across = owner.shape
    block_count = down * across
    blocks, kept, halfway = left.at[pl.ds(0, block_count)], left.at[pl.ds(block_count, block_count)], right
    d, m = lax.axis_index("dp"), lax.axis_index("mp")
    x, y = lax.rem(m, SIDE), m // SIDE

    def at(displacement):
        return lax.rem(y + displacement[1], SIDE) * SIDE + lax.rem(x + displacement[0], SIDE)

    expert = m * columns // (columns * SIDE)
    own_features = pl.ds(pl.multiple_of(d * rows, rows), rows)
    own_words = pl.ds(pl.multiple_of(d * (rows // 16), rows // 16), rows // 16)
    barrier = pltpu.get_barrier_semaphore()
    for step in range(1, mp_size):
        pl.semaphore_signal(barrier, inc=1, device_id=(d, lax.rem(m + step, mp_size)), device_id_type=MESH)
    for step in range(1, dp_size):
        pl.semaphore_signal(barrier, inc=1, device_id=(lax.rem(d + step, dp_size), m), device_id_type=MESH)

    root_loads = [
        pltpu.make_async_copy(left_hbm, left, load_sem.at[0]),
        pltpu.make_async_copy(right_hbm, right, load_sem.at[1]),
    ]
    own_loads = [
        pltpu.make_async_copy(hidden_hbm.at[expert, :, own_features], hidden.at[d], load_sem.at[2]),
        pltpu.make_async_copy(grads_hbm, grads.at[d], load_sem.at[3]),
        pltpu.make_async_copy(words_hbm.at[own_words], words, load_sem.at[4]),
    ]
    for load in root_loads + own_loads:
        load.start()

    targets = [owner[j // across, j % across] for j in range(block_count)]
    for j in range(block_count):
        tile[0, j] = targets[j]

    def clear(j, carry):
        tile[0, j] = jnp.int32(-1)
        return carry

    lax.fori_loop(block_count, LANES, clear, 0)
    row = lax.broadcasted_iota(jnp.int32, (HALF, HALF), 0)
    column = lax.broadcasted_iota(jnp.int32, (HALF, HALF), 1)
    for k, test in enumerate((row >= column, row < column, row > column, row == column)):
        triangles[k] = jnp.where(test, 1.0, 0.0).astype(jnp.bfloat16)
    pl.semaphore_wait(barrier, mp_size - 1 + dp_size - 1)

    for displacement in FAR + [legs[0] for legs in RELAYED] + DIAGONAL + STRAIGHT + NEAR:
        pltpu.make_async_remote_copy(
            src_ref=tile, dst_ref=lists.at[m], send_sem=list_send.at[0], recv_sem=list_recv.at[0],
            device_id=(d, at(displacement)), device_id_type=MESH,
        ).start()
    for j in range(block_count):
        lists[m, 0, j] = targets[j]

    gathers = []
    for step in range(1, dp_size):
        peer = lax.rem(d + step, dp_size)
        features = pl.ds(pl.multiple_of(peer * rows, rows), rows)
        for which, (source, sink) in enumerate((
            (hidden_hbm.at[expert, :, features], hidden.at[d]),
            (grads_hbm, grads.at[d]),
        )):
            copy = pltpu.make_async_remote_copy(
                src_ref=source, dst_ref=sink, send_sem=gather_send.at[which, step], recv_sem=gather_recv.at[which, step],
                device_id=(peer, m), device_id_type=MESH,
            )
            copy.start()
            gathers.append(copy)

    others = lists.at[pl.ds(0, mp_size - 1)]
    pltpu.make_async_copy(others, others, list_recv.at[0]).wait()
    for slot, displacement in enumerate(ORDER):
        sender = at((SIDE - displacement[0], SIDE - displacement[1]))
        block = jnp.int32(0)
        for j in range(1, block_count):
            block = jnp.where(targets[j] == sender, jnp.int32(j), block)
        block_of_slot[slot] = block

    def rank_step(sender, taken):
        ranks[sender] = jnp.minimum(taken, capacity - 1)
        hit = jnp.int32(0)
        for j in range(block_count):
            hit = jnp.where(lists[sender, 0, j] == m, jnp.int32(1), hit)
        return taken + hit

    lax.fori_loop(0, mp_size, rank_step, jnp.int32(0))
    for load in root_loads:
        load.wait()

    def pack(displacement, halves=(1, 0)):
        slot = SLOT[displacement]
        rank = ranks[at(displacement)]
        for q in halves:
            root = (left, right)[q]
            b = root[rank, 0:HALF, HALF:BLOCK]
            mixed = root[rank, 0:HALF, 0:HALF] * triangles[0] + root[rank, HALF:BLOCK, HALF:BLOCK] * triangles[1]
            base = q * 4 * HALF
            for half in range(2):
                lanes = slice(half * LANES, (half + 1) * LANES)
                send_slots[slot, base + half * HALF : base + (half + 1) * HALF, :] = b[:, lanes]
                send_slots[slot, base + (2 + half) * HALF : base + (3 + half) * HALF, :] = mixed[:, lanes]
        if 1 in halves:
            place = lax.broadcasted_iota(jnp.int32, (16, LANES), 0)
            extra = jnp.zeros((16, LANES), jnp.float32)
            for q, root in enumerate((left, right)):
                last = (root[rank, HALF:BLOCK, HALF:BLOCK] * triangles[3]).astype(jnp.float32)
                diagonal = jnp.sum(last, axis=0, keepdims=True)
                for half in range(2):
                    extra = jnp.where(place == 2 * q + half, diagonal[:, half * LANES : (half + 1) * LANES], extra)
            send_slots[slot, SLOT_ROWS - 16 : SLOT_ROWS, :] = extra.astype(jnp.bfloat16)

    parts = [pl.ds(BLOCK * HALF // LANES, SLOT_ROWS - BLOCK * HALF // LANES), pl.ds(0, BLOCK * HALF // LANES)]
    hops = [[], []]
    for p, part in enumerate(parts):
        for k, (displacement, first, second) in enumerate(RELAYED):
            pack(displacement, (1 - p,))
            copy = pltpu.make_async_remote_copy(
                src_ref=send_slots.at[SLOT[displacement], part], dst_ref=relay_slots.at[k, part],
                send_sem=hop_send.at[p, k], recv_sem=hop_recv.at[p, k], device_id=(d, at(first)), device_id_type=MESH,
            )
            copy.start()
            hops[p].append(copy)
    sends = []
    for displacement in NEAR + DIAGONAL + FAR + STRAIGHT:
        pack(displacement)
        slot = SLOT[displacement]
        copy = pltpu.make_async_remote_copy(
            src_ref=send_slots.at[slot], dst_ref=slots.at[slot],
            send_sem=slot_send.at[slot], recv_sem=slot_recv.at[slot], device_id=(d, at(displacement)), device_id_type=MESH,
        )
        copy.start()
        sends.append(copy)
    pack((0, 0))
    pltpu.make_async_copy(send_slots.at[0], slots.at[0], slot_recv.at[0]).start()
    forwards = []
    for p, part in enumerate(parts):
        for k, (displacement, first, second) in enumerate(RELAYED):
            hops[p][k].wait_recv()
            slot = SLOT[displacement]
            copy = pltpu.make_async_remote_copy(
                src_ref=relay_slots.at[k, part], dst_ref=slots.at[slot, part],
                send_sem=last_send.at[p, k], recv_sem=last_recv.at[p, k], device_id=(d, at(second)), device_id_type=MESH,
            )
            copy.start()
            forwards.append(copy)

    for load in own_loads:
        load.wait()
    for copy in gathers:
        copy.wait()

    def gradient_step(j, carry):
        features = pl.ds(pl.multiple_of(j // across * BLOCK, BLOCK), BLOCK)
        places = pl.ds(pl.multiple_of(lax.rem(j, across) * BLOCK, BLOCK), BLOCK)
        gradient = lax.dot_general(
            hidden[:, :, features].reshape(-1, BLOCK), grads[:, :, places].reshape(-1, BLOCK),
            (((0,), (0,)), ((), ())), preferred_element_type=jnp.float32,
        )
        in_words = pl.ds(pl.multiple_of(j // across * (BLOCK // 16), BLOCK // 16), BLOCK // 16)
        keep = jnp.where(kept_rows(words[in_words, places]), 1.0, 0.0)
        kept[j] = keep.astype(jnp.bfloat16)
        block = (gradient * keep).astype(jnp.bfloat16)
        blocks[j] = block
        wide = block.astype(jnp.float32)
        norms[j] = jnp.sum(wide * wide)
        return carry

    lax.fori_loop(0, block_count, gradient_step, 0)

    def unpack(slot, q, full):
        base = q * 4 * HALF
        part = lambda k: slots[slot, base + k * HALF : base + (k + 1) * HALF, :]
        b = jnp.concatenate([part(0), part(1)], axis=1)
        mixed = jnp.concatenate([part(2), part(3)], axis=1)
        extra = slots[slot, SLOT_ROWS - 16 : SLOT_ROWS, :].astype(jnp.float32)
        diagonal = jnp.concatenate([extra[2 * q : 2 * q + 1, :], extra[2 * q + 1 : 2 * q + 2, :]], axis=1)
        turned = mixed.T
        full[0:HALF, 0:HALF] = mixed * triangles[0] + turned * triangles[1]
        full[0:HALF, HALF:BLOCK] = b
        full[HALF:BLOCK, 0:HALF] = b.T
        full[HALF:BLOCK, HALF:BLOCK] = (
            mixed * triangles[1] + turned * triangles[2] + triangles[3] * diagonal.astype(jnp.bfloat16)
        )

    def apply_right(slot):
        unpack(slot, 1, right_full)
        block = blocks[block_of_slot[slot]]
        return jnp.dot(block, right_full[...], preferred_element_type=jnp.float32).astype(jnp.bfloat16)

    def scale(slot, preconditioned):
        j = block_of_slot[slot]
        count = BLOCK * BLOCK
        numerator = jnp.sqrt(norms[j] / count)
        denominator = jnp.sqrt(jnp.sum(preconditioned * preconditioned) / count + 1e-06)
        scaled_out[slot] = (preconditioned * (numerator / denominator)).astype(jnp.bfloat16) * kept[j]

    def finish(slot, right_applied):
        unpack(slot, 0, left_full)
        scale(slot, jnp.dot(left_full[...], right_applied, preferred_element_type=jnp.float32))

    def direct_step(slot, carry):
        pltpu.make_async_copy(send_slots.at[slot], slots.at[slot], slot_recv.at[slot]).wait()
        finish(slot, apply_right(slot))
        return carry

    def right_step(k, carry):
        part = parts[0]
        pltpu.make_async_copy(send_slots.at[k, part], relay_slots.at[k, part], last_recv.at[0, k]).wait()
        halfway[k] = apply_right(k + DIRECT)
        return carry

    def left_step(pair, carry):
        part = parts[1]
        both = ((2 * pair, left_full), (2 * pair + 1, right_full))
        products = []
        for k, full in both:
            pltpu.make_async_copy(send_slots.at[k, part], relay_slots.at[k, part], last_recv.at[1, k]).wait()
            unpack(k + DIRECT, 0, full)
            products.append(jnp.dot(full[...], halfway[k], preferred_element_type=jnp.float32))
        for (k, _), product in zip(both, products):
            scale(k + DIRECT, product)
        return carry

    lax.fori_loop(0, DIRECT, direct_step, 0)
    lax.fori_loop(0, len(RELAYED), right_step, 0)
    pltpu.make_async_copy(others, others, list_send.at[0]).wait()
    for copy in hops[0] + hops[1] + sends:
        copy.wait_send()
    lax.fori_loop(0, len(RELAYED) // 2, left_step, 0)
    for copy in forwards:
        copy.wait_send()


def place_kernel(owner, scaled, out, sem):
    down, across = owner.shape
    m = lax.axis_index("mp")
    copies = []
    for j in range(down * across):
        target = owner[j // across, j % across]
        away_x = lax.rem(lax.rem(m, SIDE) - lax.rem(target, SIDE) + SIDE, SIDE)
        away_y = lax.rem(m // SIDE - target // SIDE + SIDE, SIDE)
        away = away_y * SIDE + away_x
        slot = lax.rem(away, 8) * 4
        slot = jnp.bitwise_and(jnp.where(
            away < 8, lax.shift_right_logical(jnp.int32(SLOT_CODES[0]), slot), lax.shift_right_logical(jnp.int32(SLOT_CODES[1]), slot)
        ), 15)
        rows = pl.ds(j // across * BLOCK, BLOCK)
        columns = pl.ds(j % across * BLOCK, BLOCK)
        copies.append(pltpu.make_async_copy(scaled.at[slot], out.at[rows, columns], sem.at[j]))
        copies[-1].start()
    for copy in copies:
        copy.wait()


def body(dp_size, mp_size, hidden, out_grads, mask_words, owner, left_root, right_root):
    tokens, columns = out_grads.shape
    rows = hidden.shape[2] // dp_size
    block_count = owner.size
    any_space = pl.BlockSpec(memory_space=pl.ANY)
    in_hbm = pl.BlockSpec(memory_space=pltpu.HBM)
    in_smem = pl.BlockSpec(memory_space=pltpu.SMEM)
    blocks = pltpu.VMEM((block_count, BLOCK, BLOCK), jnp.bfloat16)
    slots = pltpu.VMEM((mp_size, SLOT_ROWS, LANES), jnp.bfloat16)
    full = pltpu.VMEM((BLOCK, BLOCK), jnp.bfloat16)
    scaled = pl.pallas_call(
        functools.partial(exchange_kernel, rows, columns, dp_size, mp_size),
        out_shape=pltpu.VMEM((mp_size, BLOCK, BLOCK), jnp.bfloat16),
        in_specs=[in_smem] + [in_hbm] * 5,
        out_specs=pl.BlockSpec(memory_space=pltpu.VMEM),
        scratch_shapes=[
            pltpu.VMEM(left_root.shape, jnp.bfloat16),
            pltpu.VMEM(right_root.shape, jnp.bfloat16),
            slots,
            pltpu.VMEM((len(RELAYED), SLOT_ROWS, LANES), jnp.bfloat16),
            slots,
            pltpu.VMEM((dp_size, tokens, rows), jnp.bfloat16),
            pltpu.VMEM((dp_size, tokens, columns), jnp.bfloat16),
            pltpu.VMEM((rows // 16, columns), jnp.int32),
            full,
            full,
            pltpu.VMEM((4, HALF, HALF), jnp.bfloat16),
            pltpu.SMEM((1, LANES), jnp.int32),
            pltpu.SMEM((mp_size, 1, LANES), jnp.int32),
            pltpu.SMEM((mp_size,), jnp.int32),
            pltpu.SMEM((mp_size,), jnp.int32),
            pltpu.SMEM((block_count,), jnp.float32),
            pltpu.SemaphoreType.DMA((6,)),
            pltpu.SemaphoreType.DMA((1,)),
            pltpu.SemaphoreType.DMA((1,)),
            pltpu.SemaphoreType.DMA((mp_size,)),
            pltpu.SemaphoreType.DMA((mp_size,)),
            pltpu.SemaphoreType.DMA((2, len(RELAYED))),
            pltpu.SemaphoreType.DMA((2, len(RELAYED))),
            pltpu.SemaphoreType.DMA((2, len(RELAYED))),
            pltpu.SemaphoreType.DMA((2, len(RELAYED))),
            pltpu.SemaphoreType.DMA((2, dp_size)),
            pltpu.SemaphoreType.DMA((2, dp_size)),
        ],
        compiler_params=pltpu.CompilerParams(
            collective_id=0, has_side_effects=True, vmem_limit_bytes=58458112
        ),
        name="exchange",
    )(owner, left_root, right_root, hidden, out_grads, mask_words)
    return pl.pallas_call(
        place_kernel,
        out_shape=jax.ShapeDtypeStruct((rows, columns), jnp.bfloat16),
        in_specs=[in_smem, any_space],
        out_specs=any_space,
        scratch_shapes=[
            pltpu.SemaphoreType.DMA((block_count,)),
        ],
        compiler_params=pltpu.CompilerParams(vmem_limit_bytes=2**20),
        name="place",
    )(owner, scaled)


def solution(mesh):
    in_specs = (
        P(None, "dp", None),
        P("dp", "mp"),
        P(None, "mp"),
        P("dp", "mp"),
        P(("dp", "mp"), None, None),
        P(("dp", "mp"), None, None),
    )
    return jax.shard_map(
        functools.partial(body, mesh.shape["dp"], mesh.shape["mp"]),
        mesh=mesh, in_specs=in_specs, out_specs=P("dp", "mp"), check_vma=False,
    )
```
